256 devices in a mesh: space: 8 (over x, core), work: 32 (over y, z).
Axes of the slice: x: 4, y: 4, z: 8, core: 2. Of those that a mesh axis runs over, the one named last changes fastest.
Arguments:
- adjoint: float32 [3, 19, 16, 32, 128], P(None, None, 'space', 'work'), may hold values from -6 to 6
- velocity: bfloat16 [3, 16, 32, 128], P(None, 'space', 'work'), may hold values from -0.29882812 to 0.29882812
- relaxation: float32 [3], replicated, may hold values from 0.6 to 1.8
- uptake: float32 [3], replicated, may hold values from 0.5 to 2
- fluid_mask: int32 [16, 32, 128], P('space', 'work'), may hold values 0 or 1
- block_cells: int32 [8, 32, 32, 4, 128], P('space', 'work'), may hold values from 0 to 255
- owner_load: int32 [8, 32, 32], P('space', 'work'), may hold values from 0 to 4, as said below
- response: bfloat16 [8, 32, 32, 4, 128, 128], P('space', 'work'), may hold values from -1 to 1
Outputs:
- rewound: float32 [3, 19, 16, 32, 128], P(None, None, 'space', 'work')
The draws below stay inside these ranges and needn't reach their ends.
Inputs may be any that keep to these rules, and one draw needn't show every extreme that they name: `owner_load`: in every space group one owner receives 4 live slots from every brick.
All inputs are finite; a program needn't handle non-finite values. No bound on the sum of `fluid_mask` on one device may be relied on, other than what follows from the above.
Results may differ from the reference program's by a relative error of at most 0.0038.
Values may be sent and summed in bfloat16 or wider, within the bound.
No kernel may reach another device: no remote copies, remote signals or barrier semaphores. Data moves between devices by JAX's collectives and lax.ppermute only.
A program may use at most 64 MiB of HBM per device.

```python
import math
import jax
import jax.numpy as jnp
from jax import lax

CX = 2
CY = 1
NZ = 128
SPECIES = 3
BLOCK = 128
CAPB = 4
STEPS = 2
NX = 16
NY = 32
N_SPACE = 8
N_WORK = 32


def draw_owner_load(key, part):
    key = jax.random.fold_in(key, 11)
    floor_key, spread_key, heavy_key = jax.random.split(key, 3)
    floor_level = jax.random.randint(floor_key, (N_SPACE, 1, N_WORK), 0, CAPB + 1)
    spread = jax.random.randint(spread_key, (N_SPACE, N_WORK, N_WORK), 0, CAPB + 1)
    counts = floor_level + spread * (CAPB - floor_level + 1) // (CAPB + 1)
    heavy = jax.random.randint(heavy_key, (N_SPACE, 1, 1), 0, N_WORK)
    owners = jax.lax.broadcasted_iota(jnp.int32, (N_SPACE, N_WORK, N_WORK), 2)
    return jnp.where(owners == heavy, CAPB, counts).astype(jnp.int32)


def draw_response(key, part):
    key = jax.random.fold_in(key, 23)
    diag_key, spread_key = jax.random.split(key, 2)
    shape = (N_SPACE, N_WORK, N_WORK, CAPB, BLOCK, BLOCK)
    spread = jax.random.normal(spread_key, shape, jnp.float32) * (0.5 / math.sqrt(BLOCK))
    diagonal = jax.random.uniform(diag_key, shape[:-1] + (1,), jnp.float32, 0.5, 1.0)
    rows = jax.lax.broadcasted_iota(jnp.int32, (BLOCK, BLOCK), 0)
    columns = jax.lax.broadcasted_iota(jnp.int32, (BLOCK, BLOCK), 1)
    return jnp.where(rows == columns, diagonal, spread).astype(jnp.bfloat16)


def set_ends(entries, key, low, high):
    shape = entries.shape
    index_at = [jax.random.randint(jax.random.fold_in(key, axis), (), 0, shape[axis]) for axis in range(len(shape))]
    entries = entries.at[tuple(index_at)].set(low)
    longest = shape.index(max(shape))
    index_at[longest] = (index_at[longest] + 1) % shape[longest]
    return entries.at[tuple(index_at)].set(high)


def shard_levels(rng, dims, cuts, least, high):
    factor_of = 1.0
    for dim, shards_of in cuts:
        steps = jax.random.uniform(jax.random.fold_in(jax.random.fold_in(rng, 6), dim), (shards_of,), jnp.float32, least / len(cuts), high / len(cuts))
        factor_of = factor_of * jnp.repeat(jnp.exp(steps), dims[dim] // shards_of).reshape((-1,) + (1,) * (len(dims) - 1 - dim))
    return factor_of


def noise(own_key, dims, scale, bound, cuts=(), held_as=jnp.bfloat16):
    level = shard_levels(own_key, dims, cuts, -0.22, 0.18) if cuts else 1.0
    drawn = jax.random.normal(own_key, dims, jnp.float32) * scale * level
    return jnp.minimum(jnp.maximum(drawn, -bound), bound).astype(held_as)


def setup_inputs(seed: int = 0) -> dict:
    streams_of = jax.random.split(jax.random.key(seed), 9)
    adjoint = noise(streams_of[0], (SPECIES, 19, NX, NY, NZ), 1.0, 6.0, ((2, 8), (3, 32)), jnp.float32)
    velocity = noise(streams_of[1], (3, NX, NY, NZ), 0.08, 0.29882812, ((1, 8), (2, 32)))
    relaxation = jnp.clip(jnp.exp(jax.random.uniform(streams_of[2], (SPECIES,), jnp.float32, math.log(0.6), math.log(1.8))), 0.6, 1.8)
    uptake = jnp.clip(jnp.exp(jax.random.uniform(streams_of[3], (SPECIES,), jnp.float32, math.log(0.5), math.log(2.0))), 0.5, 2.0)
    fluid_mask = set_ends((jax.random.randint(streams_of[4], (NX, NY, NZ), 0, 4) < 3).astype(jnp.int32), jax.random.fold_in(streams_of[4], 1), 0, 1)
    block_cells = set_ends(jax.random.randint(streams_of[5], (N_SPACE, N_WORK, N_WORK, CAPB, BLOCK), 0, CX * CY * NZ), jax.random.fold_in(streams_of[5], 1), 0, (CX * CY * NZ) - 1).astype(jnp.int32)
    owner_load = draw_owner_load(jax.random.fold_in(streams_of[8], 71), 0)
    response = draw_response(jax.random.fold_in(streams_of[8], 71), 0)
    return dict(adjoint=adjoint, velocity=velocity, relaxation=relaxation, uptake=uptake, fluid_mask=fluid_mask, block_cells=block_cells, owner_load=owner_load, response=response)


DIRECTIONS = ((0, 0, 0), (1, 0, 0), (-1, 0, 0), (0, 1, 0), (0, -1, 0), (0, 0, 1), (0, 0, -1),
              (1, 1, 0), (-1, -1, 0), (1, -1, 0), (-1, 1, 0), (1, 0, 1), (-1, 0, -1), (1, 0, -1), (-1, 0, 1),
              (0, 1, 1), (0, -1, -1), (0, 1, -1), (0, -1, 1))
WEIGHTS = (1.0 / 3.0,) + (1.0 / 18.0,) * 6 + (1.0 / 36.0,) * 12


def select_moves(padded, width_x, width_y):
    pieces = []
    for number, offset in enumerate(DIRECTIONS):
        sliced = padded[:, number, 1 + offset[0]:1 + offset[0] + width_x, 1 + offset[1]:1 + offset[1] + width_y, :]
        pieces.append(jnp.roll(sliced, -offset[2], axis=-1))
    return jnp.stack(pieces, axis=1)


def collide(pulled, velocity, relaxation, fluid_mask):
    speeds = velocity.astype(jnp.float32)
    density = jnp.zeros(pulled.shape[:1] + pulled.shape[2:], jnp.float32)
    for number, offset in enumerate(DIRECTIONS):
        factor = 1.0 + 3.0 * (offset[0] * speeds[0] + offset[1] * speeds[1] + offset[2] * speeds[2])
        density = density + WEIGHTS[number] * factor * pulled[:, number]
    rate_column = relaxation[:, None, None, None, None]
    keeper = fluid_mask.astype(jnp.float32)
    collided = ((1.0 - rate_column) * pulled + rate_column * density[:, None]) * keeper
    return collided, density


def couple_global(collided, density, block_cells, owner_load, response, uptake):
    species = density.shape[0]
    brick_cells = CX * CY * NZ
    bricks = density.reshape(species, N_SPACE, CX, N_WORK, CY, NZ).transpose(1, 3, 0, 2, 4, 5)
    bricks = bricks.reshape(N_SPACE, N_WORK, species, brick_cells)
    flat_cells = block_cells.reshape(N_SPACE, N_WORK, -1)
    picked = jax.vmap(jax.vmap(lambda values, places: values[:, places]))(bricks, flat_cells)
    picked = picked.reshape(N_SPACE, N_WORK, species, N_WORK, CAPB, BLOCK)
    slot_numbers = jnp.arange(CAPB, dtype=jnp.int32)
    occupied = (slot_numbers[None, None, None, :] < owner_load[..., None]).astype(jnp.float32)
    outgoing = (picked * occupied[:, :, None, :, :, None]).astype(jnp.bfloat16)
    outgoing = lax.optimization_barrier(outgoing).astype(jnp.float32)
    incoming = jnp.swapaxes(outgoing, 1, 3)

    def per_space(pair):
        matrices, values = pair
        return jnp.einsum("qbkij,qsbkj->qsbki", matrices.astype(jnp.float32), values,
                          precision=lax.Precision.HIGHEST)

    answer = lax.map(per_space, (response, incoming))
    answer = answer * uptake[None, None, :, None, None, None]
    returned = jnp.swapaxes(answer, 1, 3).reshape(N_SPACE, N_WORK, species, -1)
    source = jax.vmap(jax.vmap(
        lambda places, values: jnp.zeros((species, brick_cells), jnp.float32).at[:, places].add(values)))(
        flat_cells, returned)
    source = source.reshape(N_SPACE, N_WORK, species, CX, CY, NZ).transpose(2, 0, 3, 1, 4, 5)
    source = source.reshape(species, NX, NY, NZ)
    weights = jnp.array(WEIGHTS, jnp.float32)
    return collided + weights[None, :, None, None, None] * source[:, None]


def reference(adjoint, velocity, relaxation, uptake, fluid_mask, block_cells, owner_load, response):
    field = adjoint
    for step_number in range(STEPS):
        padded = jnp.pad(field, ((0, 0), (0, 0), (1, 1), (1, 1), (0, 0)))
        pulled = select_moves(padded, NX, NY)
        collided, density = collide(pulled, velocity, relaxation, fluid_mask)
        field = couple_global(collided, density, block_cells, owner_load, response, uptake)
    return field
```

```python
import jax
import jax.numpy as jnp
from jax import lax
from jax.experimental import pallas as pl
from jax.experimental.pallas import tpu as pltpu
from jax.sharding import PartitionSpec as P

DIRECTIONS = (
    (0, 0, 0),
    (1, 0, 0),
    (-1, 0, 0),
    (0, 1, 0),
    (0, -1, 0),
    (0, 0, 1),
    (0, 0, -1),
    (1, 1, 0),
    (-1, -1, 0),
    (1, -1, 0),
    (-1, 1, 0),
    (1, 0, 1),
    (-1, 0, -1),
    (1, 0, -1),
    (-1, 0, 1),
    (0, 1, 1),
    (0, -1, -1),
    (0, 1, -1),
    (0, -1, 1),
)
WEIGHTS = (1.0 / 3.0,) + (1.0 / 18.0,) * 6 + (1.0 / 36.0,) * 12
INDEX = {c: i for i, c in enumerate(DIRECTIONS)}

MIDDLE = ((0, 0, 0), (0, 0, 1), (0, 0, -1), (0, 1, 0), (0, 1, 1), (0, 1, -1), (0, -1, 0), (0, -1, 1), (0, -1, -1))
PLUS = ((1, 0, 0), (1, 0, 1), (1, 0, -1), (1, 1, 0), (1, -1, 0))
MINUS = ((-1, 0, 0), (-1, 0, 1), (-1, 0, -1), (-1, 1, 0), (-1, -1, 0))
PLACE = {c: n for n, c in enumerate(MIDDLE)}
PLACE.update({c: n for n, c in enumerate(PLUS)})
PLACE.update({c: n for n, c in enumerate(MINUS)})
SPECIES = 3
LANES = 128
F32 = jnp.float32
BF16 = jnp.bfloat16
CHUNKS = 4

VM = pl.BlockSpec(memory_space=pltpu.VMEM)
SM = pl.BlockSpec(memory_space=pltpu.SMEM)
HBM = pl.BlockSpec(memory_space=pl.ANY)


def tile(count, dtype=F32, rows=8):
    return jax.ShapeDtypeStruct((count, rows, LANES), dtype)


def rows_of(shape=(8, LANES)):
    return lax.broadcasted_iota(jnp.int32, shape, 0)


def half(value):
    return pltpu.roll(value, 4, 0)


def along(value, step):
    return pltpu.roll(value, (-step) % LANES, 1) if step else value


def per_species(ref):
    species = rows_of() % 4
    out = jnp.zeros((8, LANES), F32)
    for s in range(SPECIES):
        out = jnp.where(species == s, ref[s], out)
    return out


def mask_tile(mask_ref):
    keep = mask_ref[:].astype(F32)
    return jnp.where(rows_of() < 4, keep[0:1], keep[1:2])


def speed_tiles(velocity_ref):
    speeds = velocity_ref[:].astype(F32)
    low = rows_of() < 4
    return [jnp.where(low, speeds[2 * c : 2 * c + 1], speeds[2 * c + 1 : 2 * c + 2]) for c in range(3)]


def moment(pulled, speeds):
    density = None
    for c, value in pulled.items():
        factor = 1.0
        drift = None
        for axis in range(3):
            if c[axis]:
                part = speeds[axis] if c[axis] > 0 else -speeds[axis]
                drift = part if drift is None else drift + part
        weight = WEIGHTS[INDEX[c]]
        term = value * weight if drift is None else value * (weight + (3.0 * weight) * drift)
        density = term if density is None else density + term
    return density


def edges():
    a = lax.axis_index("space")
    b = lax.axis_index("work")
    return (a < lax.axis_size("space") - 1, a > 0, b < lax.axis_size("work") - 1, b > 0)


def arrange_kernel(field_ref, mask_ref, middle_ref, plus_ref, minus_ref):
    keep = mask_ref[:].astype(F32)
    for group, ref in ((MIDDLE, middle_ref), (PLUS, plus_ref), (MINUS, minus_ref)):
        for n, c in enumerate(group):
            for x in range(2):
                ref[n, 4 * x : 4 * x + 3, :] = field_ref[pl.ds(INDEX[c] * 2 + x, SPECIES, stride=38), :]
                ref[n, 4 * x + 3 : 4 * x + 4, :] = keep[x : x + 1]


def across_kernel(middle_ref, plus_ref, minus_ref, right_ref, left_ref, up_ref, down_ref):
    has_right, has_left, _, _ = edges()
    for sign, ref in ((1, up_ref), (-1, down_ref)):
        for n, cz in enumerate((0, 1, -1)):
            ref[n] = middle_ref[PLACE[(0, sign, cz)]]
        p = PLACE[(1, sign, 0)]
        ref[3] = plus_ref[p]
        ref[4] = jnp.where(has_right, right_ref[p], 0.0)
        p = PLACE[(-1, sign, 0)]
        ref[5] = minus_ref[p]
        ref[6] = jnp.where(has_left, left_ref[p], 0.0)


def write_payload(payload_ref, density, cells_ref, load_ref):
    high = density.astype(BF16).astype(F32)
    low = density - high
    rows = rows_of()
    for q in range(payload_ref.shape[0]):
        load = load_ref[q]
        cells = cells_ref[4 * q : 4 * q + 4, :].astype(F32)
        live = [jnp.where(k < load, cells[k : k + 1], -1.0) for k in range(4)]
        top = jnp.where(rows == 3, live[0], jnp.where(rows == 7, live[1], high))
        bottom = jnp.where(rows == 3, live[2], jnp.where(rows == 7, live[3], low))
        payload_ref[q] = jnp.concatenate([top, bottom], axis=0).astype(BF16)


def first_kernel(
    middle_ref, plus_ref, minus_ref, right_ref, left_ref, above_ref, below_ref,
    velocity_ref, mask_ref, cells_ref, relaxation_ref, load_ref,
    stay_ref, up_ref, down_ref, gain_ref, payload_ref,
):
    has_right, has_left, has_above, has_below = edges()
    first_half = rows_of() < 4
    rate = per_species(relaxation_ref)
    keep = mask_tile(mask_ref)
    right = [jnp.where(has_right, right_ref[n], 0.0) for n in range(5)]
    left = [jnp.where(has_left, left_ref[n], 0.0) for n in range(5)]
    above = [jnp.where(has_above, above_ref[n], 0.0) for n in range(7)]
    below = [jnp.where(has_below, below_ref[n], 0.0) for n in range(7)]
    pulled = {}
    for cz in (0, 1, -1):
        pulled[(0, 0, cz)] = along(middle_ref[PLACE[(0, 0, cz)]], cz)
        p = PLACE[(1, 0, cz)]
        pulled[(1, 0, cz)] = along(jnp.where(first_half, half(plus_ref[p]), half(right[p])), cz)
        p = PLACE[(-1, 0, cz)]
        pulled[(-1, 0, cz)] = along(jnp.where(first_half, half(left[p]), half(minus_ref[p])), cz)
    for sign, side in ((1, above), (-1, below)):
        for n, cz in enumerate((0, 1, -1)):
            pulled[(0, sign, cz)] = along(side[n], cz)
        pulled[(1, sign, 0)] = jnp.where(first_half, half(side[3]), half(side[4]))
        pulled[(-1, sign, 0)] = jnp.where(first_half, half(side[6]), half(side[5]))
    pulled = {c: pulled[c] for c in DIRECTIONS if c in pulled}
    density = moment(pulled, speed_tiles(velocity_ref))
    write_payload(payload_ref, density, cells_ref, load_ref)

    kept = 1.0 - rate
    right_mask = jnp.where(first_half, keep[4:5], right[0][3:4])
    left_mask = jnp.where(first_half, left[0][7:8], keep[0:1])
    here, to_right, to_left = (keep * kept, right_mask * kept, left_mask * kept)
    for n, cz in enumerate((0, 1, -1)):
        stay_ref[n] = here * pulled[(0, 0, cz)]
        stay_ref[3 + n] = to_right * along(right[PLACE[(1, 0, cz)]], cz)
        stay_ref[6 + n] = to_left * along(left[PLACE[(-1, 0, cz)]], cz)
    for sign, side, ref in ((1, above, up_ref), (-1, below, down_ref)):
        for n, cz in enumerate((0, 1, -1)):
            ref[n] = here * pulled[(0, sign, cz)]
        ref[3] = to_right * side[4]
        ref[4] = to_left * side[6]
    for n, side in enumerate((below, None, above)):
        if side is None:
            gain_ref[n] = keep * rate
        else:
            gain_ref[n] = jnp.where(first_half, side[0][3:4], side[0][7:8]) * rate
    gain_ref[3] = density


def owner_kernel(incoming_ref, response_ref, out_ref, matrices_ref, sums_ref, done, *, fold):
    count = incoming_ref.shape[0]
    each = count // CHUNKS
    copies = [
        pltpu.make_async_copy(
            response_ref.at[pl.ds(n * each, each)], matrices_ref.at[pl.ds(n * each, each)], done.at[n]
        )
        for n in range(CHUNKS)
    ]
    for copy in copies:
        copy.start()
    if fold:
        out_ref[0, 16:24, :] = jnp.zeros((8, LANES), BF16)
        out_ref[count - 1, 24:32, :] = jnp.zeros((8, LANES), BF16)
    first_half = rows_of() < 4
    cell_rows = lax.broadcasted_iota(jnp.int32, (LANES, LANES), 0)
    contract = (((1,), (1,)), ((), ()))

    def one(b):
        tiles = incoming_ref[b].astype(F32)
        top = tiles[0:8]
        lefts = []
        rights = []
        for k, row in enumerate((3, 7, 11, 15)):
            cell = tiles[row : row + 1].astype(jnp.int32)
            lane = cell & (LANES - 1)
            second = jnp.broadcast_to(cell >> 7, (8, LANES))
            mine = second == jnp.where(first_half, 0, 1)
            found = jnp.take_along_axis(
                top, jnp.broadcast_to(lane, (8, LANES)), axis=1, mode="promise_in_bounds"
            )
            picked = jnp.where(mine, found, half(found)).astype(BF16)
            reply = lax.dot_general(picked, matrices_ref[b, k], contract, preferred_element_type=F32)
            reply = jnp.where(mine, reply, 0.0)
            high = reply.astype(BF16).astype(F32)
            lefts.append(jnp.concatenate([high, reply - high], axis=0).astype(BF16))
            rights.append(jnp.where(cell_rows == lane, 1.0, 0.0).astype(BF16))
        both = lax.dot_general(
            jnp.concatenate(lefts, axis=1), jnp.concatenate(rights, axis=1), contract, preferred_element_type=F32
        )
        total = both[0:8] + both[8:16]
        high = total.astype(BF16).astype(F32)
        out_ref[b, 0:16, :] = jnp.concatenate([high, total - high], axis=0).astype(BF16)
        sums_ref[b] = total

    for n in range(CHUNKS):
        copies[n].wait()

        def group(g, carry):
            for u in range(4):
                one(n * each + g * 4 + u)
            return carry

        lax.fori_loop(0, each // 4, group, 0)
    if fold:
        zero = jnp.zeros((8, LANES), F32)
        for b in range(count):
            before = sums_ref[b - 1] if b > 0 else zero
            after = sums_ref[b + 1] if b < count - 1 else zero
            out_ref[b, 16:32, :] = jnp.concatenate([before, after], axis=0).astype(BF16)


def total_of(returned_ref, rows):
    total = returned_ref[0, 0:rows, :].astype(F32)
    for q in range(1, returned_ref.shape[0]):
        total = total + returned_ref[q, 0:rows, :].astype(F32)
    return total


def gather_kernel(returned_ref, incoming_ref, gain_ref, uptake_ref, parts_ref, right_ref, left_ref):
    first_half = rows_of() < 4
    factor = per_species(uptake_ref)
    total = total_of(returned_ref, 32)
    sources = (total[16:24], total[0:8] + total[8:16], total[24:32])
    b = lax.axis_index("work")
    last = lax.axis_size("work") - 1
    for n, source in enumerate(sources):
        source = factor * source
        if n == 1:
            density = gain_ref[3]
        else:
            tiles = incoming_ref[jnp.clip(b + n - 1, 0, last)].astype(F32)
            density = tiles[0:8] + tiles[8:16]
        equilibrium = gain_ref[n] * density
        parts_ref[n] = equilibrium
        parts_ref[3 + n] = source
        right_ref[n] = jnp.where(first_half, equilibrium, half(source))
        left_ref[n] = jnp.where(first_half, half(equilibrium), source)


def second_kernel(
    stay_ref, above_ref, below_ref, parts_ref, right_ref, left_ref,
    velocity_ref, cells_ref, load_ref,
    pulled_ref, density_ref, payload_ref,
):
    has_right, has_left, has_above, has_below = edges()
    first_half = rows_of() < 4
    pulled = {}
    for n, cy in enumerate((-1, 0, 1)):
        equilibrium, source = (parts_ref[n], parts_ref[3 + n])
        right = jnp.where(has_right, right_ref[n], 0.0)
        left = jnp.where(has_left, left_ref[n], 0.0)
        moved = {
            0: (equilibrium, source),
            1: (jnp.where(first_half, half(equilibrium), half(right)), jnp.where(first_half, half(source), right)),
            -1: (jnp.where(first_half, left, half(equilibrium)), jnp.where(first_half, half(left), half(source))),
        }
        for c in DIRECTIONS:
            if c[1] != cy:
                continue
            shifted, added = moved[c[0]]
            if cy == 0:
                base = stay_ref[(0, 3, 6)[c[0]] + (0, 1, 2)[c[2]]]
            else:
                inside, ref = (has_above, above_ref) if cy > 0 else (has_below, below_ref)
                base = ref[(0, 1, 2)[c[2]] if c[0] == 0 else (3 if c[0] > 0 else 4)]
                base = jnp.where(inside, base, 0.0)
            pulled[c] = along(base + shifted + WEIGHTS[INDEX[c]] * added, c[2])
    pulled = {c: pulled[c] for c in DIRECTIONS}
    density = moment(pulled, speed_tiles(velocity_ref))
    write_payload(payload_ref, density, cells_ref, load_ref)
    for i, c in enumerate(DIRECTIONS):
        pulled_ref[i] = pulled[c]
    density_ref[0] = density


def last_kernel(returned_ref, pulled_ref, density_ref, mask_ref, relaxation_ref, uptake_ref, out_ref):
    total = total_of(returned_ref, 16)
    source = per_species(uptake_ref) * (total[0:8] + total[8:16])
    rate = per_species(relaxation_ref)
    keep = mask_tile(mask_ref)
    shared = keep * rate * density_ref[0]
    here = keep * (1.0 - rate)
    for i in range(len(DIRECTIONS)):
        value = here * pulled_ref[i] + shared + WEIGHTS[i] * source
        for x in range(2):
            out_ref[pl.ds(i * 2 + x, SPECIES, stride=38), :] = value[4 * x : 4 * x + 3]


def call(kernel, out_shape, in_specs, name, **rest):
    single = not isinstance(out_shape, (tuple, list))
    return pl.pallas_call(
        kernel,
        out_shape=out_shape,
        in_specs=in_specs,
        out_specs=VM if single else tuple(VM for _ in out_shape),
        name=name,
        compiler_params=pltpu.CompilerParams(vmem_limit_bytes=32 * 1024 * 1024),
        **rest,
    )


def body(adjoint, velocity, relaxation, uptake, fluid_mask, block_cells, owner_load, response):
    columns = lax.axis_size("space")
    owners = lax.axis_size("work")
    field = adjoint.reshape(-1, LANES)
    speeds = velocity.reshape(-1, LANES)
    mask = fluid_mask.reshape(-1, LANES)
    cells = block_cells.reshape(-1, LANES)
    load = owner_load.reshape(-1)
    matrices = response.reshape(response.shape[2:])

    def to_lower(value, axis, count):
        return lax.ppermute(value, axis, [((i + 1) % count, i) for i in range(count)])

    def to_upper(value, axis, count):
        return lax.ppermute(value, axis, [(i, (i + 1) % count) for i in range(count)])

    def owner(incoming, fold):
        return call(
            lambda *refs: owner_kernel(*refs, fold=fold),
            jax.ShapeDtypeStruct((owners, 32 if fold else 16, LANES), BF16),
            [VM, HBM],
            "owner_fold" if fold else "owner",
            scratch_shapes=[
                pltpu.VMEM(matrices.shape, BF16),
                pltpu.VMEM((owners, 8, LANES), F32),
                pltpu.SemaphoreType.DMA((CHUNKS,)),
            ],
        )(incoming, matrices)

    def exchange(value):
        return lax.all_to_all(value, "work", split_axis=0, concat_axis=0, tiled=True)

    payload_shape = jax.ShapeDtypeStruct((owners, 16, LANES), BF16)
    middle, plus, minus = call(arrange_kernel, (tile(9), tile(5), tile(5)), [VM] * 2, "arrange")(field, mask)
    right = to_lower(plus, "space", columns)
    left = to_upper(minus, "space", columns)
    up, down = call(across_kernel, (tile(7), tile(7)), [VM] * 5, "across")(middle, plus, minus, right, left)
    above = to_lower(up, "work", owners)
    below = to_upper(down, "work", owners)
    stay, up, down, gain, payload = call(
        first_kernel, (tile(9), tile(5), tile(5), tile(4), payload_shape), [VM] * 10 + [SM] * 2, "first"
    )(middle, plus, minus, right, left, above, below, speeds, mask, cells, relaxation, load)
    incoming = exchange(payload)
    above = to_lower(up, "work", owners)
    below = to_upper(down, "work", owners)
    returned = exchange(owner(incoming, True))
    parts, right, left = call(gather_kernel, (tile(6), tile(3), tile(3)), [VM] * 3 + [SM], "gather")(
        returned, incoming, gain, uptake
    )
    right = to_lower(right, "space", columns)
    left = to_upper(left, "space", columns)
    pulled, density, payload = call(
        second_kernel, (tile(19), tile(1), payload_shape), [VM] * 8 + [SM], "second"
    )(stay, above, below, parts, right, left, speeds, cells, load)
    returned = exchange(owner(exchange(payload), False))
    out = call(last_kernel, jax.ShapeDtypeStruct(field.shape, F32), [VM] * 4 + [SM] * 2, "last")(
        returned, pulled, density, mask, relaxation, uptake
    )
    return out.reshape(adjoint.shape)


def solution(mesh):
    placed = (
        P(None, None, "space", "work", None),
        P(None, "space", "work", None),
        P(),
        P(),
        P("space", "work", None),
        P("space", "work", None, None, None),
        P("space", "work", None),
        P("space", "work", None, None, None, None),
    )
    return jax.shard_map(
        body,
        mesh=mesh,
        in_specs=placed,
        out_specs=P(None, None, "space", "work", None),
        check_vma=False,
    )
```

```python
import jax
import jax.numpy as jnp
from jax import lax
from jax.experimental import pallas as pl
from jax.experimental.pallas import tpu as pltpu
from jax.sharding import PartitionSpec as P

DIRECTIONS = (
    (0, 0, 0),
    (1, 0, 0),
    (-1, 0, 0),
    (0, 1, 0),
    (0, -1, 0),
    (0, 0, 1),
    (0, 0, -1),
    (1, 1, 0),
    (-1, -1, 0),
    (1, -1, 0),
    (-1, 1, 0),
    (1, 0, 1),
    (-1, 0, -1),
    (1, 0, -1),
    (-1, 0, 1),
    (0, 1, 1),
    (0, -1, -1),
    (0, 1, -1),
    (0, -1, 1),
)
WEIGHTS = (1.0 / 3.0,) + (1.0 / 18.0,) * 6 + (1.0 / 36.0,) * 12
INDEX = {c: i for i, c in enumerate(DIRECTIONS)}

MIDDLE = ((0, 0, 0), (0, 0, 1), (0, 0, -1), (0, 1, 0), (0, 1, 1), (0, 1, -1), (0, -1, 0), (0, -1, 1), (0, -1, -1))
PLUS = ((1, 0, 0), (1, 0, 1), (1, 0, -1), (1, 1, 0), (1, -1, 0))
MINUS = ((-1, 0, 0), (-1, 0, 1), (-1, 0, -1), (-1, 1, 0), (-1, -1, 0))
PLACE = {c: n for n, c in enumerate(MIDDLE)}
PLACE.update({c: n for n, c in enumerate(PLUS)})
PLACE.update({c: n for n, c in enumerate(MINUS)})
SPECIES = 3
LANES = 128
F32 = jnp.float32
BF16 = jnp.bfloat16
CHUNKS = 4

VM = pl.BlockSpec(memory_space=pltpu.VMEM)
SM = pl.BlockSpec(memory_space=pltpu.SMEM)
HBM = pl.BlockSpec(memory_space=pltpu.HBM)


def tile(count, dtype=F32, rows=8):
    return jax.ShapeDtypeStruct((count, rows, LANES), dtype)


def rows_of(shape=(8, LANES)):
    return lax.broadcasted_iota(jnp.int32, shape, 0)


def half(value):
    return pltpu.roll(value, 4, 0)


def along(value, step):
    return pltpu.roll(value, (-step) % LANES, 1) if step else value


def per_species(ref):
    species = rows_of() % 4
    out = jnp.zeros((8, LANES), F32)
    for s in range(SPECIES):
        out = jnp.where(species == s, ref[s], out)
    return out


def moment(pulled, speeds):
    density = None
    for c, value in pulled.items():
        factor = 1.0
        drift = None
        for axis in range(3):
            if c[axis]:
                part = speeds[axis] if c[axis] > 0 else -speeds[axis]
                drift = part if drift is None else drift + part
        weight = WEIGHTS[INDEX[c]]
        term = value * weight if drift is None else value * (weight + (3.0 * weight) * drift)
        density = term if density is None else density + term
    return density


def edges():
    a = lax.axis_index("space")
    b = lax.axis_index("work")
    return (a < lax.axis_size("space") - 1, a > 0, b < lax.axis_size("work") - 1, b > 0)


def is_even(axis):
    return lax.axis_index(axis) % 2 == 0


def arrange_kernel(
    field_hbm, velocity_hbm, mask_hbm, relaxation_ref, uptake_ref,
    middle_ref, near_ref, far_ref, fixed_ref,
    field_ref, velocity_ref, mask_ref, plus_ref, minus_ref, done,
):
    pairs = ((field_hbm, field_ref), (velocity_hbm, velocity_ref), (mask_hbm, mask_ref))
    copies = [pltpu.make_async_copy(source, target, done.at[n]) for n, (source, target) in enumerate(pairs)]
    for copy in copies:
        copy.start()
    for copy in copies:
        copy.wait()
    first_half = rows_of() < 4
    keep = [mask_ref[x].astype(F32) for x in range(2)]
    for group, ref in ((MIDDLE, middle_ref), (PLUS, plus_ref), (MINUS, minus_ref)):
        for n, c in enumerate(group):
            for x in range(2):
                for s in range(SPECIES):
                    row = 4 * x + s
                    ref[n, row : row + 1, :] = field_ref[s, INDEX[c], x]
                ref[n, 4 * x + 3 : 4 * x + 4, :] = keep[x]
    even = is_even("space")
    for n in range(5):
        plus, minus = (plus_ref[n], minus_ref[n])
        near_ref[n] = jnp.where(even, minus, plus)
        far_ref[n] = jnp.where(even, plus, minus)
    fixed_ref[0] = per_species(relaxation_ref)
    fixed_ref[1] = per_species(uptake_ref)
    fixed_ref[2] = jnp.where(first_half, keep[0], keep[1])
    for c in range(3):
        speeds = velocity_ref[c, 0].astype(F32)
        fixed_ref[3 + c] = jnp.where(first_half, speeds[0:1], speeds[1:2])


def slots_kernel(cells_hbm, load_hbm, slots_ref, cells_ref, load_ref, done):
    pairs = ((cells_hbm, cells_ref), (load_hbm, load_ref))
    copies = [pltpu.make_async_copy(source, target, done.at[n]) for n, (source, target) in enumerate(pairs)]
    for copy in copies:
        copy.start()
    for copy in copies:
        copy.wait()
    rows = rows_of()
    for q in range(slots_ref.shape[0]):
        load = load_ref[0, 0, q]
        cells = cells_ref[0, 0, q].astype(F32)
        live = [jnp.where(k < load, cells[k : k + 1], -1.0) for k in range(4)]
        for n in range(2):
            slots_ref[q, 8 * n : 8 * n + 8, :] = jnp.where(
                rows == 3, live[2 * n], jnp.where(rows == 7, live[2 * n + 1], 0.0)
            )


def across_kernel(middle_ref, near_ref, far_ref, first_ref, second_ref, one_ref, two_ref):
    has_right, has_left, _, _ = edges()
    even = is_even("space")
    even_row = is_even("work")
    pieces = {}
    for sign in (1, -1):
        p, m = (PLACE[(1, sign, 0)], PLACE[(-1, sign, 0)])
        pieces[sign] = [middle_ref[PLACE[(0, sign, cz)]] for cz in (0, 1, -1)] + [
            jnp.where(even, far_ref[p], near_ref[p]),
            jnp.where(has_right, jnp.where(even, first_ref[p], second_ref[p]), 0.0),
            jnp.where(even, near_ref[m], far_ref[m]),
            jnp.where(has_left, jnp.where(even, second_ref[m], first_ref[m]), 0.0),
        ]
    for n in range(7):
        one_ref[n] = jnp.where(even_row, pieces[-1][n], pieces[1][n])
        two_ref[n] = jnp.where(even_row, pieces[1][n], pieces[-1][n])


def write_payload(payload_ref, density, slots_ref):
    live = rows_of() % 4 < SPECIES
    high = density.astype(BF16).astype(F32)
    both = jnp.concatenate([jnp.where(live, high, 0.0), jnp.where(live, density - high, 0.0)], axis=0)
    for q in range(payload_ref.shape[0]):
        payload_ref[q] = (both + slots_ref[q]).astype(BF16)


def first_kernel(
    middle_ref, near_ref, far_ref, first_ref, second_ref, one_ref, two_ref, fixed_ref, slots_ref,
    stay_ref, third_ref, fourth_ref, gain_ref, payload_ref,
):
    has_right, has_left, has_above, has_below = edges()
    even = is_even("space")
    even_row = is_even("work")
    first_half = rows_of() < 4
    rate = fixed_ref[0]
    keep = fixed_ref[2]
    plus = [jnp.where(even, far_ref[n], near_ref[n]) for n in range(3)]
    minus = [jnp.where(even, near_ref[n], far_ref[n]) for n in range(3)]
    right = [jnp.where(has_right, jnp.where(even, first_ref[n], second_ref[n]), 0.0) for n in range(3)]
    left = [jnp.where(has_left, jnp.where(even, second_ref[n], first_ref[n]), 0.0) for n in range(3)]
    above = [jnp.where(has_above, jnp.where(even_row, one_ref[n], two_ref[n]), 0.0) for n in range(7)]
    below = [jnp.where(has_below, jnp.where(even_row, two_ref[n], one_ref[n]), 0.0) for n in range(7)]
    pulled = {}
    for n, cz in enumerate((0, 1, -1)):
        pulled[(0, 0, cz)] = along(middle_ref[PLACE[(0, 0, cz)]], cz)
        pulled[(1, 0, cz)] = along(jnp.where(first_half, half(plus[n]), half(right[n])), cz)
        pulled[(-1, 0, cz)] = along(jnp.where(first_half, half(left[n]), half(minus[n])), cz)
    for sign, side in ((1, above), (-1, below)):
        for n, cz in enumerate((0, 1, -1)):
            pulled[(0, sign, cz)] = along(side[n], cz)
        pulled[(1, sign, 0)] = jnp.where(first_half, half(side[3]), half(side[4]))
        pulled[(-1, sign, 0)] = jnp.where(first_half, half(side[6]), half(side[5]))
    pulled = {c: pulled[c] for c in DIRECTIONS}
    density = moment(pulled, [fixed_ref[3 + c] for c in range(3)])
    write_payload(payload_ref, density, slots_ref)

    kept = 1.0 - rate
    right_mask = jnp.where(first_half, keep[4:5], right[0][3:4])
    left_mask = jnp.where(first_half, left[0][7:8], keep[0:1])
    here, to_right, to_left = (keep * kept, right_mask * kept, left_mask * kept)
    for n, cz in enumerate((0, 1, -1)):
        stay_ref[n] = here * pulled[(0, 0, cz)]
        stay_ref[3 + n] = to_right * along(right[n], cz)
        stay_ref[6 + n] = to_left * along(left[n], cz)
    sends = {}
    for sign, side in ((1, above), (-1, below)):
        sends[sign] = [here * pulled[(0, sign, cz)] for cz in (0, 1, -1)] + [to_right * side[4], to_left * side[6]]
    for n in range(5):
        third_ref[n] = jnp.where(even_row, sends[-1][n], sends[1][n])
        fourth_ref[n] = jnp.where(even_row, sends[1][n], sends[-1][n])
    gain_ref[0] = jnp.where(first_half, below[0][3:4], below[0][7:8]) * rate
    gain_ref[1] = keep * rate
    gain_ref[2] = jnp.where(first_half, above[0][3:4], above[0][7:8]) * rate
    gain_ref[3] = density


def owner_kernel(incoming_ref, response_ref, out_ref, matrices_ref, picked_ref, reply_ref, sums_ref, done, *, fold):
    count = incoming_ref.shape[0]
    each = count // CHUNKS
    copies = [
        pltpu.make_async_copy(
            response_ref.at[pl.ds(n * each, each)], matrices_ref.at[pl.ds(n * each, each)], done.at[n]
        )
        for n in range(CHUNKS)
    ]
    for copy in copies:
        copy.start()
    column = jnp.where(rows_of() < 4, 0, 1)
    cell_rows = lax.broadcasted_iota(jnp.int32, (LANES, LANES), 0)
    contract = (((1,), (1,)), ((), ()))
    zero = jnp.zeros((8, LANES), F32)
    slot_rows = (3, 7, 11, 15)
    for b in range(count):
        tiles = incoming_ref[b].astype(F32)
        top = tiles[0:8]
        picked = []
        for row in slot_rows:
            cell = jnp.broadcast_to(tiles[row : row + 1].astype(jnp.int32), (8, LANES))
            found = jnp.take_along_axis(top, cell & (LANES - 1), axis=1, mode="promise_in_bounds")
            picked.append(jnp.where((cell >> 7) == column, found, half(found)))
        upper = jnp.concatenate([picked[0], zero, picked[2], zero], axis=0)
        lower = jnp.concatenate([zero, picked[1], zero, picked[3]], axis=0)
        picked_ref[b] = jnp.concatenate([upper, lower], axis=1).astype(BF16)
    for n in range(CHUNKS):
        copies[n].wait()
        for b in range(n * each, (n + 1) * each):
            top = jnp.concatenate([matrices_ref[b, 0], matrices_ref[b, 1]], axis=1)
            bottom = jnp.concatenate([matrices_ref[b, 2], matrices_ref[b, 3]], axis=1)
            grid = jnp.concatenate([top, bottom], axis=0)
            reply = lax.dot_general(picked_ref[b], grid, contract, preferred_element_type=F32)
            reply_ref[b] = jnp.concatenate([reply[0:16, 0:LANES], reply[16:32, LANES:]], axis=0)
    for b in range(count):
        tiles = incoming_ref[b].astype(F32)
        lefts = []
        rights = []
        for k, row in enumerate(slot_rows):
            cell = tiles[row : row + 1].astype(jnp.int32)
            mine = jnp.broadcast_to(cell >> 7, (8, LANES)) == column
            reply = jnp.where(mine, reply_ref[b, 8 * k : 8 * k + 8, :], 0.0)
            high = reply.astype(BF16).astype(F32)
            lefts.append(jnp.concatenate([high, reply - high], axis=0).astype(BF16))
            rights.append(jnp.where(cell_rows == (cell & (LANES - 1)), 1.0, 0.0).astype(BF16))
        both = lax.dot_general(
            jnp.concatenate(lefts, axis=1), jnp.concatenate(rights, axis=1), contract, preferred_element_type=F32
        )
        total = both[0:8] + both[8:16]
        high = total.astype(BF16).astype(F32)
        out_ref[b, 0:16, :] = jnp.concatenate([high, total - high], axis=0).astype(BF16)
        if fold:
            sums_ref[b] = total
    if fold:
        for b in range(count):
            before = sums_ref[b - 1] if b > 0 else zero
            after = sums_ref[b + 1] if b < count - 1 else zero
            out_ref[b, 16:32, :] = jnp.concatenate([before, after], axis=0).astype(BF16)


def total_of(returned_ref, rows):
    total = returned_ref[0, 0:rows, :].astype(F32)
    for q in range(1, returned_ref.shape[0]):
        total = total + returned_ref[q, 0:rows, :].astype(F32)
    return total


def gather_kernel(returned_ref, incoming_ref, gain_ref, fixed_ref, parts_ref, near_ref, far_ref):
    first_half = rows_of() < 4
    factor = fixed_ref[1]
    total = total_of(returned_ref, 32)
    sources = (total[16:24], total[0:8] + total[8:16], total[24:32])
    b = lax.axis_index("work")
    last = lax.axis_size("work") - 1
    even = is_even("space")
    for n, source in enumerate(sources):
        source = factor * source
        if n == 1:
            density = gain_ref[3]
        else:
            tiles = incoming_ref[jnp.clip(b + n - 1, 0, last)].astype(F32)
            density = tiles[0:8] + tiles[8:16]
        equilibrium = gain_ref[n] * density
        parts_ref[n] = equilibrium
        parts_ref[3 + n] = source
        to_lower = jnp.where(first_half, equilibrium, half(source))
        to_upper = jnp.where(first_half, half(equilibrium), source)
        near_ref[n] = jnp.where(even, to_upper, to_lower)
        far_ref[n] = jnp.where(even, to_lower, to_upper)


def second_kernel(
    stay_ref, third_ref, fourth_ref, parts_ref, first_ref, second_ref, fixed_ref, slots_ref,
    pulled_ref, density_ref, payload_ref,
):
    has_right, has_left, has_above, has_below = edges()
    even = is_even("space")
    even_row = is_even("work")
    first_half = rows_of() < 4
    above = [jnp.where(has_above, jnp.where(even_row, third_ref[n], fourth_ref[n]), 0.0) for n in range(5)]
    below = [jnp.where(has_below, jnp.where(even_row, fourth_ref[n], third_ref[n]), 0.0) for n in range(5)]
    pulled = {}
    for n, cy in enumerate((-1, 0, 1)):
        equilibrium, source = (parts_ref[n], parts_ref[3 + n])
        right = jnp.where(has_right, jnp.where(even, first_ref[n], second_ref[n]), 0.0)
        left = jnp.where(has_left, jnp.where(even, second_ref[n], first_ref[n]), 0.0)
        moved = {
            0: (equilibrium, source),
            1: (jnp.where(first_half, half(equilibrium), half(right)), jnp.where(first_half, half(source), right)),
            -1: (jnp.where(first_half, left, half(equilibrium)), jnp.where(first_half, half(left), half(source))),
        }
        for c in DIRECTIONS:
            if c[1] != cy:
                continue
            shifted, added = moved[c[0]]
            if cy == 0:
                base = stay_ref[{0: 0, 1: 3, -1: 6}[c[0]] + {0: 0, 1: 1, -1: 2}[c[2]]]
            else:
                side = above if cy > 0 else below
                base = side[{0: {0: 0, 1: 1, -1: 2}[c[2]], 1: 3, -1: 4}[c[0]]]
            pulled[c] = along(base + shifted + WEIGHTS[INDEX[c]] * added, c[2])
    pulled = {c: pulled[c] for c in DIRECTIONS}
    density = moment(pulled, [fixed_ref[3 + c] for c in range(3)])
    write_payload(payload_ref, density, slots_ref)
    for i, c in enumerate(DIRECTIONS):
        pulled_ref[i] = pulled[c]
    density_ref[0] = density


def last_kernel(returned_ref, pulled_ref, density_ref, fixed_ref, out_ref):
    total = total_of(returned_ref, 16)
    rate = fixed_ref[0]
    keep = fixed_ref[2]
    source = fixed_ref[1] * (total[0:8] + total[8:16])
    shared = keep * rate * density_ref[0]
    here = keep * (1.0 - rate)
    for i in range(len(DIRECTIONS)):
        value = here * pulled_ref[i] + shared + WEIGHTS[i] * source
        for x in range(2):
            for s in range(SPECIES):
                row = 4 * x + s
                out_ref[s, i, x] = value[row : row + 1]


def call(kernel, out_shape, in_specs, name, **rest):
    single = not isinstance(out_shape, (tuple, list))
    return pl.pallas_call(
        kernel,
        out_shape=out_shape,
        in_specs=in_specs,
        out_specs=VM if single else tuple(VM for _ in out_shape),
        name=name,
        compiler_params=pltpu.CompilerParams(vmem_limit_bytes=32 * 1024 * 1024),
        **rest,
    )


def swapped(value, axis, odd):
    count = lax.axis_size(axis)
    step = [(1 if (i % 2 == 0) != odd else -1) for i in range(count)]
    return lax.ppermute(value, axis, [(i, (i + step[i]) % count) for i in range(count)])


def body(adjoint, velocity, relaxation, uptake, fluid_mask, block_cells, owner_load, response):
    owners = lax.axis_size("work")
    matrices = response.reshape(response.shape[2:])
    speeds = velocity.transpose(0, 2, 1, 3)

    def both_ways(near, far, axis):
        return swapped(near, axis, False), swapped(far, axis, True)

    def owner(incoming, fold):
        return call(
            lambda *refs: owner_kernel(*refs, fold=fold),
            jax.ShapeDtypeStruct((owners, 32 if fold else 16, LANES), BF16),
            [VM, HBM],
            "owner_fold" if fold else "owner",
            scratch_shapes=[
                pltpu.VMEM(matrices.shape, BF16),
                pltpu.VMEM((owners, 32, 2 * LANES), BF16),
                pltpu.VMEM((owners, 32, LANES), F32),
                pltpu.VMEM((owners, 8, LANES), F32),
                pltpu.SemaphoreType.DMA((CHUNKS,)),
            ],
        )(incoming, matrices)

    def exchange(value):
        return lax.all_to_all(value, "work", split_axis=0, concat_axis=0, tiled=True)

    payload_shape = jax.ShapeDtypeStruct((owners, 16, LANES), BF16)
    middle, near, far, fixed = call(
        arrange_kernel,
        (tile(9), tile(5), tile(5), tile(6)),
        [HBM] * 3 + [SM] * 2,
        "arrange",
        scratch_shapes=[
            pltpu.VMEM(adjoint.shape, F32),
            pltpu.VMEM(speeds.shape, BF16),
            pltpu.VMEM(fluid_mask.shape, jnp.int32),
            pltpu.VMEM((5, 8, LANES), F32),
            pltpu.VMEM((5, 8, LANES), F32),
            pltpu.SemaphoreType.DMA((3,)),
        ],
    )(adjoint, speeds, fluid_mask, relaxation, uptake)
    first, second = both_ways(near, far, "space")
    slots = call(
        slots_kernel,
        tile(owners, rows=16),
        [HBM] * 2,
        "slots",
        scratch_shapes=[
            pltpu.VMEM(block_cells.shape, jnp.int32),
            pltpu.SMEM(owner_load.shape, jnp.int32),
            pltpu.SemaphoreType.DMA((2,)),
        ],
    )(block_cells, owner_load)
    one, two = call(across_kernel, (tile(7), tile(7)), [VM] * 5, "across")(middle, near, far, first, second)
    one, two = both_ways(one, two, "work")
    stay, third, fourth, gain, payload = call(
        first_kernel, (tile(9), tile(5), tile(5), tile(4), payload_shape), [VM] * 9, "first"
    )(middle, near, far, first, second, one, two, fixed, slots)
    incoming = exchange(payload)
    third, fourth = both_ways(third, fourth, "work")
    returned = exchange(owner(incoming, True))
    parts, near, far = call(gather_kernel, (tile(6), tile(3), tile(3)), [VM] * 4, "gather")(
        returned, incoming, gain, fixed
    )
    first, second = both_ways(near, far, "space")
    pulled, density, payload = call(
        second_kernel, (tile(19), tile(1), payload_shape), [VM] * 8, "second"
    )(stay, third, fourth, parts, first, second, fixed, slots)
    returned = exchange(owner(exchange(payload), False))
    return call(last_kernel, jax.ShapeDtypeStruct(adjoint.shape, F32), [VM] * 4, "last")(
        returned, pulled, density, fixed
    )


def solution(mesh):
    placed = (
        P(None, None, "space", "work", None),
        P(None, "space", "work", None),
        P(),
        P(),
        P("space", "work", None),
        P("space", "work", None, None, None),
        P("space", "work", None),
        P("space", "work", None, None, None, None),
    )
    return jax.shard_map(
        body,
        mesh=mesh,
        in_specs=placed,
        out_specs=P(None, None, "space", "work", None),
        check_vma=False,
    )
```

```python
import jax
import jax.numpy as jnp
from jax import lax
from jax.experimental import pallas as pl
from jax.experimental.pallas import tpu as pltpu
from jax.sharding import PartitionSpec as P

DIRECTIONS = (
    (0, 0, 0),
    (1, 0, 0),
    (-1, 0, 0),
    (0, 1, 0),
    (0, -1, 0),
    (0, 0, 1),
    (0, 0, -1),
    (1, 1, 0),
    (-1, -1, 0),
    (1, -1, 0),
    (-1, 1, 0),
    (1, 0, 1),
    (-1, 0, -1),
    (1, 0, -1),
    (-1, 0, 1),
    (0, 1, 1),
    (0, -1, -1),
    (0, 1, -1),
    (0, -1, 1),
)
WEIGHTS = (1.0 / 3.0,) + (1.0 / 18.0,) * 6 + (1.0 / 36.0,) * 12
INDEX = {c: i for i, c in enumerate(DIRECTIONS)}

MIDDLE = ((0, 0, 0), (0, 0, 1), (0, 0, -1), (0, 1, 0), (0, 1, 1), (0, 1, -1), (0, -1, 0), (0, -1, 1), (0, -1, -1))
PLUS = ((1, 0, 0), (1, 0, 1), (1, 0, -1), (1, 1, 0), (1, -1, 0))
MINUS = ((-1, 0, 0), (-1, 0, 1), (-1, 0, -1), (-1, 1, 0), (-1, -1, 0))
PLACE = {c: n for n, c in enumerate(MIDDLE)}
PLACE.update({c: n for n, c in enumerate(PLUS)})
PLACE.update({c: n for n, c in enumerate(MINUS)})
SPECIES = 3
LANES = 128
F32 = jnp.float32
BF16 = jnp.bfloat16
CHUNKS = 4

VM = pl.BlockSpec(memory_space=pltpu.VMEM)
SM = pl.BlockSpec(memory_space=pltpu.SMEM)
HBM = pl.BlockSpec(memory_space=pltpu.HBM)


def tile(count, dtype=F32, rows=8):
    return jax.ShapeDtypeStruct((count, rows, LANES), dtype)


def rows_of(shape=(8, LANES)):
    return lax.broadcasted_iota(jnp.int32, shape, 0)


def half(value):
    return pltpu.roll(value, 4, 0)


def along(value, step):
    return pltpu.roll(value, (-step) % LANES, 1) if step else value


def per_species(ref):
    species = rows_of() % 4
    out = jnp.zeros((8, LANES), F32)
    for s in range(SPECIES):
        out = jnp.where(species == s, ref[s], out)
    return out


def moment(pulled, speeds):
    density = None
    for c, value in pulled.items():
        factor = 1.0
        drift = None
        for axis in range(3):
            if c[axis]:
                part = speeds[axis] if c[axis] > 0 else -speeds[axis]
                drift = part if drift is None else drift + part
        weight = WEIGHTS[INDEX[c]]
        term = value * weight if drift is None else value * (weight + (3.0 * weight) * drift)
        density = term if density is None else density + term
    return density


def edges():
    a = lax.axis_index("space")
    b = lax.axis_index("work")
    return (a < lax.axis_size("space") - 1, a > 0, b < lax.axis_size("work") - 1, b > 0)


def is_even(axis):
    return lax.axis_index(axis) % 2 == 0


def arrange_kernel(
    field_hbm, velocity_hbm, mask_hbm, relaxation_hbm, uptake_hbm,
    middle_ref, near_ref, far_ref, fixed_ref,
    field_ref, velocity_ref, mask_ref, relaxation_ref, uptake_ref, plus_ref, minus_ref, done,
):
    pairs = (
        (field_hbm, field_ref),
        (velocity_hbm, velocity_ref),
        (mask_hbm, mask_ref),
        (relaxation_hbm, relaxation_ref),
        (uptake_hbm, uptake_ref),
    )
    copies = [pltpu.make_async_copy(source, target, done.at[n]) for n, (source, target) in enumerate(pairs)]
    for copy in copies:
        copy.start()
    for copy in copies:
        copy.wait()
    first_half = rows_of() < 4
    keep = [mask_ref[x].astype(F32) for x in range(2)]
    for group, ref in ((MIDDLE, middle_ref), (PLUS, plus_ref), (MINUS, minus_ref)):
        for n, c in enumerate(group):
            for x in range(2):
                for s in range(SPECIES):
                    row = 4 * x + s
                    ref[n, row : row + 1, :] = field_ref[s, INDEX[c], x]
                ref[n, 4 * x + 3 : 4 * x + 4, :] = keep[x]
    even = is_even("space")
    for n in range(5):
        plus, minus = (plus_ref[n], minus_ref[n])
        near_ref[n] = jnp.where(even, minus, plus)
        far_ref[n] = jnp.where(even, plus, minus)
    fixed_ref[0] = per_species(relaxation_ref)
    fixed_ref[1] = per_species(uptake_ref)
    fixed_ref[2] = jnp.where(first_half, keep[0], keep[1])
    for c in range(3):
        speeds = velocity_ref[c, 0].astype(F32)
        fixed_ref[3 + c] = jnp.where(first_half, speeds[0:1], speeds[1:2])


def start_fetch(response_hbm, response_ref, done):
    parts = done.shape[0]
    each = response_hbm.shape[0] // parts
    copies = [
        pltpu.make_async_copy(
            response_hbm.at[pl.ds(n * each, each)], response_ref.at[pl.ds(n * each, each)], done.at[n]
        )
        for n in range(parts)
    ]
    for copy in copies:
        copy.start()
    return copies


def fetch_kernel(response_hbm, middle_ref, response_ref, sides_ref, done):
    copies = start_fetch(response_hbm, response_ref, done)
    sides_ref[...] = middle_ref[3:9]
    for copy in copies:
        copy.wait()


def fetch_again_kernel(response_hbm, third_ref, fourth_ref, response_ref, sides_ref, done):
    copies = start_fetch(response_hbm, response_ref, done)
    _, _, has_above, has_below = edges()
    even_row = is_even("work")
    for n in range(5):
        third, fourth = (third_ref[n], fourth_ref[n])
        sides_ref[n] = jnp.where(has_above, jnp.where(even_row, third, fourth), 0.0)
        sides_ref[5 + n] = jnp.where(has_below, jnp.where(even_row, fourth, third), 0.0)
    for copy in copies:
        copy.wait()


def slots_kernel(cells_hbm, load_hbm, slots_ref, cells_ref, load_ref, done):
    pairs = ((cells_hbm, cells_ref), (load_hbm, load_ref))
    copies = [pltpu.make_async_copy(source, target, done.at[n]) for n, (source, target) in enumerate(pairs)]
    for copy in copies:
        copy.start()
    for copy in copies:
        copy.wait()
    rows = rows_of()
    for q in range(slots_ref.shape[0]):
        load = load_ref[0, 0, q]
        cells = cells_ref[0, 0, q].astype(F32)
        live = [jnp.where(k < load, cells[k : k + 1], -1.0) for k in range(4)]
        for n in range(2):
            slots_ref[q, 8 * n : 8 * n + 8, :] = jnp.where(
                rows == 3, live[2 * n], jnp.where(rows == 7, live[2 * n + 1], 0.0)
            )


def across_kernel(sides_ref, near_ref, far_ref, first_ref, second_ref, one_ref, two_ref):
    has_right, has_left, _, _ = edges()
    even = is_even("space")
    even_row = is_even("work")
    pieces = {}
    for sign in (1, -1):
        p, m = (PLACE[(1, sign, 0)], PLACE[(-1, sign, 0)])
        pieces[sign] = [sides_ref[PLACE[(0, sign, cz)] - 3] for cz in (0, 1, -1)] + [
            jnp.where(even, far_ref[p], near_ref[p]),
            jnp.where(has_right, jnp.where(even, first_ref[p], second_ref[p]), 0.0),
            jnp.where(even, near_ref[m], far_ref[m]),
            jnp.where(has_left, jnp.where(even, second_ref[m], first_ref[m]), 0.0),
        ]
    for n in range(7):
        one_ref[n] = jnp.where(even_row, pieces[-1][n], pieces[1][n])
        two_ref[n] = jnp.where(even_row, pieces[1][n], pieces[-1][n])


def write_payload(payload_ref, density, slots_ref):
    live = rows_of() % 4 < SPECIES
    high = density.astype(BF16).astype(F32)
    both = jnp.concatenate([jnp.where(live, high, 0.0), jnp.where(live, density - high, 0.0)], axis=0)
    for q in range(payload_ref.shape[0]):
        payload_ref[q] = (both + slots_ref[q]).astype(BF16)


def first_kernel(
    middle_ref, near_ref, far_ref, first_ref, second_ref, one_ref, two_ref, fixed_ref, slots_ref,
    stay_ref, third_ref, fourth_ref, gain_ref, payload_ref,
):
    has_right, has_left, has_above, has_below = edges()
    even = is_even("space")
    even_row = is_even("work")
    first_half = rows_of() < 4
    rate = fixed_ref[0]
    keep = fixed_ref[2]
    plus = [jnp.where(even, far_ref[n], near_ref[n]) for n in range(3)]
    minus = [jnp.where(even, near_ref[n], far_ref[n]) for n in range(3)]
    right = [jnp.where(has_right, jnp.where(even, first_ref[n], second_ref[n]), 0.0) for n in range(3)]
    left = [jnp.where(has_left, jnp.where(even, second_ref[n], first_ref[n]), 0.0) for n in range(3)]
    above = [jnp.where(has_above, jnp.where(even_row, one_ref[n], two_ref[n]), 0.0) for n in range(7)]
    below = [jnp.where(has_below, jnp.where(even_row, two_ref[n], one_ref[n]), 0.0) for n in range(7)]
    pulled = {}
    for n, cz in enumerate((0, 1, -1)):
        pulled[(0, 0, cz)] = along(middle_ref[PLACE[(0, 0, cz)]], cz)
        pulled[(1, 0, cz)] = along(jnp.where(first_half, half(plus[n]), half(right[n])), cz)
        pulled[(-1, 0, cz)] = along(jnp.where(first_half, half(left[n]), half(minus[n])), cz)
    for sign, side in ((1, above), (-1, below)):
        for n, cz in enumerate((0, 1, -1)):
            pulled[(0, sign, cz)] = along(side[n], cz)
        pulled[(1, sign, 0)] = jnp.where(first_half, half(side[3]), half(side[4]))
        pulled[(-1, sign, 0)] = jnp.where(first_half, half(side[6]), half(side[5]))
    pulled = {c: pulled[c] for c in DIRECTIONS}
    density = moment(pulled, [fixed_ref[3 + c] for c in range(3)])
    write_payload(payload_ref, density, slots_ref)

    kept = 1.0 - rate
    right_mask = jnp.where(first_half, keep[4:5], right[0][3:4])
    left_mask = jnp.where(first_half, left[0][7:8], keep[0:1])
    here, to_right, to_left = (keep * kept, right_mask * kept, left_mask * kept)
    for n, cz in enumerate((0, 1, -1)):
        stay_ref[n] = here * pulled[(0, 0, cz)]
        stay_ref[3 + n] = to_right * along(right[n], cz)
        stay_ref[6 + n] = to_left * along(left[n], cz)
    sends = {}
    for sign, side in ((1, above), (-1, below)):
        sends[sign] = [here * pulled[(0, sign, cz)] for cz in (0, 1, -1)] + [to_right * side[4], to_left * side[6]]
    for n in range(5):
        third_ref[n] = jnp.where(even_row, sends[-1][n], sends[1][n])
        fourth_ref[n] = jnp.where(even_row, sends[1][n], sends[-1][n])
    gain_ref[0] = jnp.where(first_half, below[0][3:4], below[0][7:8]) * rate
    gain_ref[1] = keep * rate
    gain_ref[2] = jnp.where(first_half, above[0][3:4], above[0][7:8]) * rate
    gain_ref[3] = density


def owner_kernel(incoming_ref, matrices_ref, out_ref, picked_ref, reply_ref, sums_ref, *, fold):
    count = incoming_ref.shape[0]
    column = jnp.where(rows_of() < 4, 0, 1)
    cell_rows = lax.broadcasted_iota(jnp.int32, (LANES, LANES), 0)
    contract = (((1,), (1,)), ((), ()))
    zero = jnp.zeros((8, LANES), F32)
    slot_rows = (3, 7, 11, 15)
    for b in range(count):
        tiles = incoming_ref[b].astype(F32)
        top = tiles[0:8]
        picked = []
        for row in slot_rows:
            cell = jnp.broadcast_to(tiles[row : row + 1].astype(jnp.int32), (8, LANES))
            found = jnp.take_along_axis(top, cell & (LANES - 1), axis=1, mode="promise_in_bounds")
            picked.append(jnp.where((cell >> 7) == column, found, half(found)))
        upper = jnp.concatenate([picked[0], zero, picked[2], zero], axis=0)
        lower = jnp.concatenate([zero, picked[1], zero, picked[3]], axis=0)
        picked_ref[b] = jnp.concatenate([upper, lower], axis=1).astype(BF16)

    def respond(b):
        top = jnp.concatenate([matrices_ref[b, 0], matrices_ref[b, 1]], axis=1)
        bottom = jnp.concatenate([matrices_ref[b, 2], matrices_ref[b, 3]], axis=1)
        grid = jnp.concatenate([top, bottom], axis=0)
        reply = lax.dot_general(picked_ref[b], grid, contract, preferred_element_type=F32)
        reply_ref[b] = jnp.concatenate([reply[0:16, 0:LANES], reply[16:32, LANES:]], axis=0)

    def spread(b):
        tiles = incoming_ref[b].astype(F32)
        lefts = []
        rights = []
        for k, row in enumerate(slot_rows):
            cell = tiles[row : row + 1].astype(jnp.int32)
            mine = jnp.broadcast_to(cell >> 7, (8, LANES)) == column
            reply = jnp.where(mine, reply_ref[b, 8 * k : 8 * k + 8, :], 0.0)
            high = reply.astype(BF16).astype(F32)
            lefts.append(jnp.concatenate([high, reply - high], axis=0).astype(BF16))
            rights.append(jnp.where(cell_rows == (cell & (LANES - 1)), 1.0, 0.0).astype(BF16))
        both = lax.dot_general(
            jnp.concatenate(lefts, axis=1), jnp.concatenate(rights, axis=1), contract, preferred_element_type=F32
        )
        total = both[0:8] + both[8:16]
        high = total.astype(BF16).astype(F32)
        out_ref[b, 0:16, :] = jnp.concatenate([high, total - high], axis=0).astype(BF16)
        if fold:
            sums_ref[b] = total

    for b in range(count):
        respond(b)
    for b in range(count):
        spread(b)
    if fold:
        for b in range(count):
            before = sums_ref[b - 1] if b > 0 else zero
            after = sums_ref[b + 1] if b < count - 1 else zero
            out_ref[b, 16:32, :] = jnp.concatenate([before, after], axis=0).astype(BF16)


def total_of(returned_ref, rows):
    total = returned_ref[0, 0:rows, :].astype(F32)
    for q in range(1, returned_ref.shape[0]):
        total = total + returned_ref[q, 0:rows, :].astype(F32)
    return total


def gather_kernel(returned_ref, incoming_ref, gain_ref, fixed_ref, parts_ref, near_ref, far_ref):
    first_half = rows_of() < 4
    factor = fixed_ref[1]
    total = total_of(returned_ref, 32)
    sources = (total[16:24], total[0:8] + total[8:16], total[24:32])
    b = lax.axis_index("work")
    last = lax.axis_size("work") - 1
    even = is_even("space")
    for n, source in enumerate(sources):
        source = factor * source
        if n == 1:
            density = gain_ref[3]
        else:
            tiles = incoming_ref[jnp.clip(b + n - 1, 0, last)].astype(F32)
            density = tiles[0:8] + tiles[8:16]
        equilibrium = gain_ref[n] * density
        parts_ref[n] = equilibrium
        parts_ref[3 + n] = source
        to_lower = jnp.where(first_half, equilibrium, half(source))
        to_upper = jnp.where(first_half, half(equilibrium), source)
        near_ref[n] = jnp.where(even, to_upper, to_lower)
        far_ref[n] = jnp.where(even, to_lower, to_upper)


def second_kernel(
    stay_ref, sides_ref, parts_ref, first_ref, second_ref, fixed_ref, slots_ref,
    pulled_ref, density_ref, payload_ref,
):
    has_right, has_left, _, _ = edges()
    even = is_even("space")
    first_half = rows_of() < 4
    above = [sides_ref[n] for n in range(5)]
    below = [sides_ref[5 + n] for n in range(5)]
    pulled = {}
    for n, cy in enumerate((-1, 0, 1)):
        equilibrium, source = (parts_ref[n], parts_ref[3 + n])
        right = jnp.where(has_right, jnp.where(even, first_ref[n], second_ref[n]), 0.0)
        left = jnp.where(has_left, jnp.where(even, second_ref[n], first_ref[n]), 0.0)
        moved = {
            0: (equilibrium, source),
            1: (jnp.where(first_half, half(equilibrium), half(right)), jnp.where(first_half, half(source), right)),
            -1: (jnp.where(first_half, left, half(equilibrium)), jnp.where(first_half, half(left), half(source))),
        }
        for c in DIRECTIONS:
            if c[1] != cy:
                continue
            shifted, added = moved[c[0]]
            if cy == 0:
                base = stay_ref[{0: 0, 1: 3, -1: 6}[c[0]] + {0: 0, 1: 1, -1: 2}[c[2]]]
            else:
                side = above if cy > 0 else below
                base = side[{0: {0: 0, 1: 1, -1: 2}[c[2]], 1: 3, -1: 4}[c[0]]]
            pulled[c] = along(base + shifted + WEIGHTS[INDEX[c]] * added, c[2])
    pulled = {c: pulled[c] for c in DIRECTIONS}
    density = moment(pulled, [fixed_ref[3 + c] for c in range(3)])
    write_payload(payload_ref, density, slots_ref)
    for i, c in enumerate(DIRECTIONS):
        pulled_ref[i] = pulled[c]
    density_ref[0] = density


def last_kernel(returned_ref, pulled_ref, density_ref, fixed_ref, out_ref):
    total = total_of(returned_ref, 16)
    rate = fixed_ref[0]
    keep = fixed_ref[2]
    source = fixed_ref[1] * (total[0:8] + total[8:16])
    shared = keep * rate * density_ref[0]
    here = keep * (1.0 - rate)
    for i in range(len(DIRECTIONS)):
        value = here * pulled_ref[i] + shared + WEIGHTS[i] * source
        for x in range(2):
            for s in range(SPECIES):
                row = 4 * x + s
                out_ref[s, i, x] = value[row : row + 1]


def call(kernel, out_shape, in_specs, name, **rest):
    single = not isinstance(out_shape, (tuple, list))
    return pl.pallas_call(
        kernel,
        out_shape=out_shape,
        in_specs=in_specs,
        out_specs=VM if single else tuple(VM for _ in out_shape),
        name=name,
        compiler_params=pltpu.CompilerParams(vmem_limit_bytes=32 * 1024 * 1024),
        **rest,
    )


def swapped(value, axis, odd):
    count = lax.axis_size(axis)
    step = [(1 if (i % 2 == 0) != odd else -1) for i in range(count)]
    return lax.ppermute(value, axis, [(i, (i + step[i]) % count) for i in range(count)])


def body(adjoint, velocity, relaxation, uptake, fluid_mask, block_cells, owner_load, response):
    owners = lax.axis_size("work")
    matrices = response.reshape(response.shape[2:])
    speeds = velocity.transpose(0, 2, 1, 3)

    def outside(value):
        return pltpu.with_memory_space_constraint(value, pltpu.HBM)

    def both_ways(near, far, axis):
        return swapped(near, axis, False), swapped(far, axis, True)

    def owner(incoming, fetched, fold):
        return call(
            lambda *refs: owner_kernel(*refs, fold=fold),
            jax.ShapeDtypeStruct((owners, 32 if fold else 16, LANES), BF16),
            [VM, VM],
            "owner_fold" if fold else "owner",
            scratch_shapes=[
                pltpu.VMEM((owners, 32, 2 * LANES), BF16),
                pltpu.VMEM((owners, 32, LANES), F32),
                pltpu.VMEM((owners, 8, LANES), F32),
            ],
        )(incoming, fetched)

    def exchange(value):
        return lax.all_to_all(value, "work", split_axis=0, concat_axis=0, tiled=True)

    payload_shape = jax.ShapeDtypeStruct((owners, 16, LANES), BF16)
    middle, near, far, fixed = call(
        arrange_kernel,
        (tile(9), tile(5), tile(5), tile(6)),
        [HBM] * 5,
        "arrange",
        scratch_shapes=[
            pltpu.VMEM(adjoint.shape, F32),
            pltpu.VMEM(speeds.shape, BF16),
            pltpu.VMEM(fluid_mask.shape, jnp.int32),
            pltpu.SMEM(relaxation.shape, F32),
            pltpu.SMEM(uptake.shape, F32),
            pltpu.VMEM((5, 8, LANES), F32),
            pltpu.VMEM((5, 8, LANES), F32),
            pltpu.SemaphoreType.DMA((5,)),
        ],
    )(*map(outside, (adjoint, speeds, fluid_mask, relaxation, uptake)))
    first, second = both_ways(near, far, "space")
    slots = call(
        slots_kernel,
        tile(owners, rows=16),
        [HBM] * 2,
        "slots",
        scratch_shapes=[
            pltpu.VMEM(block_cells.shape, jnp.int32),
            pltpu.SMEM(owner_load.shape, jnp.int32),
            pltpu.SemaphoreType.DMA((2,)),
        ],
    )(*map(outside, (block_cells, owner_load)))
    fetched, sides = call(
        fetch_kernel,
        (pltpu.VMEM(matrices.shape, BF16), tile(6)),
        [HBM, VM],
        "fetch",
        scratch_shapes=[pltpu.SemaphoreType.DMA((CHUNKS,))],
    )(outside(matrices), middle)
    one, two = call(across_kernel, (tile(7), tile(7)), [VM] * 5, "across")(sides, near, far, first, second)
    one, two = both_ways(one, two, "work")
    stay, third, fourth, gain, payload = call(
        first_kernel, (tile(9), tile(5), tile(5), tile(4), payload_shape), [VM] * 9, "first"
    )(middle, near, far, first, second, one, two, fixed, slots)
    incoming = exchange(payload)
    third, fourth = both_ways(third, fourth, "work")
    returned = exchange(owner(incoming, fetched, True))
    parts, near, far = call(gather_kernel, (tile(6), tile(3), tile(3)), [VM] * 4, "gather")(
        returned, incoming, gain, fixed
    )
    first, second = both_ways(near, far, "space")
    fetched, sides = call(
        fetch_again_kernel,
        (pltpu.VMEM(matrices.shape, BF16), tile(10)),
        [HBM, VM, VM],
        "fetch_again",
        scratch_shapes=[pltpu.SemaphoreType.DMA((CHUNKS,))],
    )(outside(matrices), third, fourth)
    pulled, density, payload = call(
        second_kernel, (tile(19), tile(1), payload_shape), [VM] * 7, "second"
    )(stay, sides, parts, first, second, fixed, slots)
    returned = exchange(owner(exchange(payload), fetched, False))
    return call(last_kernel, jax.ShapeDtypeStruct(adjoint.shape, F32), [VM] * 4, "last")(
        returned, pulled, density, fixed
    )


def solution(mesh):
    placed = (
        P(None, None, "space", "work", None),
        P(None, "space", "work", None),
        P(),
        P(),
        P("space", "work", None),
        P("space", "work", None, None, None),
        P("space", "work", None),
        P("space", "work", None, None, None, None),
    )
    return jax.shard_map(
        body,
        mesh=mesh,
        in_specs=placed,
        out_specs=P(None, None, "space", "work", None),
        check_vma=False,
    )
```

```python
import jax
import jax.numpy as jnp
from jax import lax
from jax.experimental import pallas as pl
from jax.experimental.pallas import tpu as pltpu
from jax.sharding import PartitionSpec as P

DIRECTIONS = (
    (0, 0, 0),
    (1, 0, 0),
    (-1, 0, 0),
    (0, 1, 0),
    (0, -1, 0),
    (0, 0, 1),
    (0, 0, -1),
    (1, 1, 0),
    (-1, -1, 0),
    (1, -1, 0),
    (-1, 1, 0),
    (1, 0, 1),
    (-1, 0, -1),
    (1, 0, -1),
    (-1, 0, 1),
    (0, 1, 1),
    (0, -1, -1),
    (0, 1, -1),
    (0, -1, 1),
)
WEIGHTS = (1.0 / 3.0,) + (1.0 / 18.0,) * 6 + (1.0 / 36.0,) * 12
INDEX = {c: i for i, c in enumerate(DIRECTIONS)}

MIDDLE = ((0, 0, 0), (0, 0, 1), (0, 0, -1), (0, 1, 0), (0, 1, 1), (0, 1, -1), (0, -1, 0), (0, -1, 1), (0, -1, -1))
PLUS = ((1, 0, 0), (1, 0, 1), (1, 0, -1), (1, 1, 0), (1, -1, 0))
MINUS = ((-1, 0, 0), (-1, 0, 1), (-1, 0, -1), (-1, 1, 0), (-1, -1, 0))
PLACE = {c: n for n, c in enumerate(MIDDLE)}
PLACE.update({c: n for n, c in enumerate(PLUS)})
PLACE.update({c: n for n, c in enumerate(MINUS)})
SPECIES = 3
LANES = 128
F32 = jnp.float32
BF16 = jnp.bfloat16
CHUNKS = 4

VM = pl.BlockSpec(memory_space=pltpu.VMEM)
SM = pl.BlockSpec(memory_space=pltpu.SMEM)
HBM = pl.BlockSpec(memory_space=pltpu.HBM)


def tile(count, dtype=F32, rows=8):
    return jax.ShapeDtypeStruct((count, rows, LANES), dtype)


def rows_of(shape=(8, LANES)):
    return lax.broadcasted_iota(jnp.int32, shape, 0)


def half(value):
    return pltpu.roll(value, 4, 0)


def along(value, step):
    return pltpu.roll(value, (-step) % LANES, 1) if step else value


def per_species(ref):
    species = rows_of() % 4
    out = jnp.zeros((8, LANES), F32)
    for s in range(SPECIES):
        out = jnp.where(species == s, ref[s], out)
    return out


def moment(pulled, speeds):
    density = None
    for c, value in pulled.items():
        factor = 1.0
        drift = None
        for axis in range(3):
            if c[axis]:
                part = speeds[axis] if c[axis] > 0 else -speeds[axis]
                drift = part if drift is None else drift + part
        weight = WEIGHTS[INDEX[c]]
        term = value * weight if drift is None else value * (weight + (3.0 * weight) * drift)
        density = term if density is None else density + term
    return density


def edges():
    a = lax.axis_index("space")
    b = lax.axis_index("work")
    return (a < lax.axis_size("space") - 1, a > 0, b < lax.axis_size("work") - 1, b > 0)


def near_is_upper(axis):
    return lax.axis_index(axis) % 2 == 1


def arrange_kernel(
    field_hbm, velocity_hbm, mask_hbm, relaxation_hbm, uptake_hbm,
    middle_ref, near_ref, far_ref, fixed_ref,
    field_ref, velocity_ref, mask_ref, relaxation_ref, uptake_ref, plus_ref, minus_ref, done,
):
    pairs = (
        (field_hbm, field_ref),
        (velocity_hbm, velocity_ref),
        (mask_hbm, mask_ref),
        (relaxation_hbm, relaxation_ref),
        (uptake_hbm, uptake_ref),
    )
    copies = [pltpu.make_async_copy(source, target, done.at[n]) for n, (source, target) in enumerate(pairs)]
    for copy in copies:
        copy.start()
    for copy in copies:
        copy.wait()
    first_half = rows_of() < 4
    keep = [mask_ref[x].astype(F32) for x in range(2)]
    for group, ref in ((MIDDLE, middle_ref), (PLUS, plus_ref), (MINUS, minus_ref)):
        for n, c in enumerate(group):
            for x in range(2):
                for s in range(SPECIES):
                    row = 4 * x + s
                    ref[n, row : row + 1, :] = field_ref[s, INDEX[c], x]
                ref[n, 4 * x + 3 : 4 * x + 4, :] = keep[x]
    upper = near_is_upper("space")
    for n in range(5):
        plus, minus = (plus_ref[n], minus_ref[n])
        near_ref[n] = jnp.where(upper, minus, plus)
        far_ref[n] = jnp.where(upper, plus, minus)
    fixed_ref[0] = per_species(relaxation_ref)
    fixed_ref[1] = per_species(uptake_ref)
    fixed_ref[2] = jnp.where(first_half, keep[0], keep[1])
    for c in range(3):
        speeds = velocity_ref[c, 0].astype(F32)
        fixed_ref[3 + c] = jnp.where(first_half, speeds[0:1], speeds[1:2])


def start_fetch(response_hbm, response_ref, done):
    parts = done.shape[0]
    each = response_hbm.shape[0] // parts
    copies = [
        pltpu.make_async_copy(
            response_hbm.at[pl.ds(n * each, each)], response_ref.at[pl.ds(n * each, each)], done.at[n]
        )
        for n in range(parts)
    ]
    for copy in copies:
        copy.start()
    return copies


def fetch_kernel(response_hbm, middle_ref, response_ref, sides_ref, done):
    copies = start_fetch(response_hbm, response_ref, done)
    sides_ref[...] = middle_ref[3:9]
    for copy in copies:
        copy.wait()


def fetch_again_kernel(response_hbm, third_ref, fourth_ref, response_ref, sides_ref, done):
    copies = start_fetch(response_hbm, response_ref, done)
    _, _, has_above, has_below = edges()
    upper_row = near_is_upper("work")
    for n in range(5):
        third, fourth = (third_ref[n], fourth_ref[n])
        sides_ref[n] = jnp.where(has_above, jnp.where(upper_row, third, fourth), 0.0)
        sides_ref[5 + n] = jnp.where(has_below, jnp.where(upper_row, fourth, third), 0.0)
    for copy in copies:
        copy.wait()


def slots_kernel(cells_hbm, load_hbm, slots_ref, cells_ref, load_ref, done):
    pairs = ((cells_hbm, cells_ref), (load_hbm, load_ref))
    copies = [pltpu.make_async_copy(source, target, done.at[n]) for n, (source, target) in enumerate(pairs)]
    for copy in copies:
        copy.start()
    for copy in copies:
        copy.wait()
    rows = rows_of()
    for q in range(slots_ref.shape[0]):
        load = load_ref[0, 0, q]
        cells = cells_ref[0, 0, q].astype(F32)
        live = [jnp.where(k < load, cells[k : k + 1], -1.0) for k in range(4)]
        for n in range(2):
            slots_ref[q, 8 * n : 8 * n + 8, :] = jnp.where(
                rows == 3, live[2 * n], jnp.where(rows == 7, live[2 * n + 1], 0.0)
            )


def across_kernel(sides_ref, near_ref, far_ref, first_ref, second_ref, one_ref, two_ref):
    has_right, has_left, _, _ = edges()
    upper = near_is_upper("space")
    upper_row = near_is_upper("work")
    pieces = {}
    for sign in (1, -1):
        p, m = (PLACE[(1, sign, 0)], PLACE[(-1, sign, 0)])
        pieces[sign] = [sides_ref[PLACE[(0, sign, cz)] - 3] for cz in (0, 1, -1)] + [
            jnp.where(upper, far_ref[p], near_ref[p]),
            jnp.where(has_right, jnp.where(upper, first_ref[p], second_ref[p]), 0.0),
            jnp.where(upper, near_ref[m], far_ref[m]),
            jnp.where(has_left, jnp.where(upper, second_ref[m], first_ref[m]), 0.0),
        ]
    for n in range(7):
        one_ref[n] = jnp.where(upper_row, pieces[-1][n], pieces[1][n])
        two_ref[n] = jnp.where(upper_row, pieces[1][n], pieces[-1][n])


def write_payload(payload_ref, density, slots_ref):
    live = rows_of() % 4 < SPECIES
    high = density.astype(BF16).astype(F32)
    both = jnp.concatenate([jnp.where(live, high, 0.0), jnp.where(live, density - high, 0.0)], axis=0)
    for q in range(payload_ref.shape[0]):
        payload_ref[q] = (both + slots_ref[q]).astype(BF16)


def first_kernel(
    middle_ref, near_ref, far_ref, first_ref, second_ref, one_ref, two_ref, fixed_ref, slots_ref,
    stay_ref, third_ref, fourth_ref, gain_ref, payload_ref,
):
    has_right, has_left, has_above, has_below = edges()
    upper = near_is_upper("space")
    upper_row = near_is_upper("work")
    first_half = rows_of() < 4
    rate = fixed_ref[0]
    keep = fixed_ref[2]
    plus = [jnp.where(upper, far_ref[n], near_ref[n]) for n in range(3)]
    minus = [jnp.where(upper, near_ref[n], far_ref[n]) for n in range(3)]
    right = [jnp.where(has_right, jnp.where(upper, first_ref[n], second_ref[n]), 0.0) for n in range(3)]
    left = [jnp.where(has_left, jnp.where(upper, second_ref[n], first_ref[n]), 0.0) for n in range(3)]
    above = [jnp.where(has_above, jnp.where(upper_row, one_ref[n], two_ref[n]), 0.0) for n in range(7)]
    below = [jnp.where(has_below, jnp.where(upper_row, two_ref[n], one_ref[n]), 0.0) for n in range(7)]
    pulled = {}
    for n, cz in enumerate((0, 1, -1)):
        pulled[(0, 0, cz)] = along(middle_ref[PLACE[(0, 0, cz)]], cz)
        pulled[(1, 0, cz)] = along(jnp.where(first_half, half(plus[n]), half(right[n])), cz)
        pulled[(-1, 0, cz)] = along(jnp.where(first_half, half(left[n]), half(minus[n])), cz)
    for sign, side in ((1, above), (-1, below)):
        for n, cz in enumerate((0, 1, -1)):
            pulled[(0, sign, cz)] = along(side[n], cz)
        pulled[(1, sign, 0)] = jnp.where(first_half, half(side[3]), half(side[4]))
        pulled[(-1, sign, 0)] = jnp.where(first_half, half(side[6]), half(side[5]))
    pulled = {c: pulled[c] for c in DIRECTIONS}
    density = moment(pulled, [fixed_ref[3 + c] for c in range(3)])
    write_payload(payload_ref, density, slots_ref)

    kept = 1.0 - rate
    right_mask = jnp.where(first_half, keep[4:5], right[0][3:4])
    left_mask = jnp.where(first_half, left[0][7:8], keep[0:1])
    here, to_right, to_left = (keep * kept, right_mask * kept, left_mask * kept)
    for n, cz in enumerate((0, 1, -1)):
        stay_ref[n] = here * pulled[(0, 0, cz)]
        stay_ref[3 + n] = to_right * along(right[n], cz)
        stay_ref[6 + n] = to_left * along(left[n], cz)
    sends = {}
    for sign, side in ((1, above), (-1, below)):
        sends[sign] = [here * pulled[(0, sign, cz)] for cz in (0, 1, -1)] + [to_right * side[4], to_left * side[6]]
    for n in range(5):
        third_ref[n] = jnp.where(upper_row, sends[-1][n], sends[1][n])
        fourth_ref[n] = jnp.where(upper_row, sends[1][n], sends[-1][n])
    gain_ref[0] = jnp.where(first_half, below[0][3:4], below[0][7:8]) * rate
    gain_ref[1] = keep * rate
    gain_ref[2] = jnp.where(first_half, above[0][3:4], above[0][7:8]) * rate
    gain_ref[3] = density


def owner_kernel(incoming_ref, matrices_ref, out_ref, picked_ref, reply_ref, sums_ref, *, fold):
    count = incoming_ref.shape[0]
    column = jnp.where(rows_of() < 4, 0, 1)
    cell_rows = lax.broadcasted_iota(jnp.int32, (LANES, LANES), 0)
    contract = (((1,), (1,)), ((), ()))
    zero = jnp.zeros((8, LANES), F32)
    slot_rows = (3, 7, 11, 15)
    for b in range(count):
        tiles = incoming_ref[b].astype(F32)
        top = tiles[0:8]
        picked = []
        for row in slot_rows:
            cell = jnp.broadcast_to(tiles[row : row + 1].astype(jnp.int32), (8, LANES))
            found = jnp.take_along_axis(top, cell & (LANES - 1), axis=1, mode="promise_in_bounds")
            picked.append(jnp.where((cell >> 7) == column, found, half(found)))
        upper = jnp.concatenate([picked[0], zero, picked[2], zero], axis=0)
        lower = jnp.concatenate([zero, picked[1], zero, picked[3]], axis=0)
        picked_ref[b] = jnp.concatenate([upper, lower], axis=1).astype(BF16)

    def respond(b):
        top = jnp.concatenate([matrices_ref[b, 0], matrices_ref[b, 1]], axis=1)
        bottom = jnp.concatenate([matrices_ref[b, 2], matrices_ref[b, 3]], axis=1)
        grid = jnp.concatenate([top, bottom], axis=0)
        reply = lax.dot_general(picked_ref[b], grid, contract, preferred_element_type=F32)
        reply_ref[b] = jnp.concatenate([reply[0:16, 0:LANES], reply[16:32, LANES:]], axis=0)

    def spread(b):
        tiles = incoming_ref[b].astype(F32)
        lefts = []
        rights = []
        for k, row in enumerate(slot_rows):
            cell = tiles[row : row + 1].astype(jnp.int32)
            mine = jnp.broadcast_to(cell >> 7, (8, LANES)) == column
            reply = jnp.where(mine, reply_ref[b, 8 * k : 8 * k + 8, :], 0.0)
            high = reply.astype(BF16).astype(F32)
            lefts.append(jnp.concatenate([high, reply - high], axis=0).astype(BF16))
            rights.append(jnp.where(cell_rows == (cell & (LANES - 1)), 1.0, 0.0).astype(BF16))
        both = lax.dot_general(
            jnp.concatenate(lefts, axis=1), jnp.concatenate(rights, axis=1), contract, preferred_element_type=F32
        )
        total = both[0:8] + both[8:16]
        high = total.astype(BF16).astype(F32)
        out_ref[b, 0:16, :] = jnp.concatenate([high, total - high], axis=0).astype(BF16)
        if fold:
            sums_ref[b] = total

    for b in range(count):
        respond(b)
    for b in range(count):
        spread(b)
    if fold:
        for b in range(count):
            before = sums_ref[b - 1] if b > 0 else zero
            after = sums_ref[b + 1] if b < count - 1 else zero
            out_ref[b, 16:32, :] = jnp.concatenate([before, after], axis=0).astype(BF16)


def total_of(returned_ref, rows):
    total = returned_ref[0, 0:rows, :].astype(F32)
    for q in range(1, returned_ref.shape[0]):
        total = total + returned_ref[q, 0:rows, :].astype(F32)
    return total


def gather_kernel(returned_ref, incoming_ref, gain_ref, fixed_ref, parts_ref, near_ref, far_ref):
    first_half = rows_of() < 4
    factor = fixed_ref[1]
    total = total_of(returned_ref, 32)
    sources = (total[16:24], total[0:8] + total[8:16], total[24:32])
    b = lax.axis_index("work")
    last = lax.axis_size("work") - 1
    upper = near_is_upper("space")
    for n, source in enumerate(sources):
        source = factor * source
        if n == 1:
            density = gain_ref[3]
        else:
            tiles = incoming_ref[jnp.clip(b + n - 1, 0, last)].astype(F32)
            density = tiles[0:8] + tiles[8:16]
        equilibrium = gain_ref[n] * density
        parts_ref[n] = equilibrium
        parts_ref[3 + n] = source
        to_lower = jnp.where(first_half, equilibrium, half(source))
        to_upper = jnp.where(first_half, half(equilibrium), source)
        near_ref[n] = jnp.where(upper, to_upper, to_lower)
        far_ref[n] = jnp.where(upper, to_lower, to_upper)


def second_kernel(
    stay_ref, sides_ref, parts_ref, first_ref, second_ref, fixed_ref, slots_ref,
    pulled_ref, density_ref, payload_ref,
):
    has_right, has_left, _, _ = edges()
    upper = near_is_upper("space")
    first_half = rows_of() < 4
    above = [sides_ref[n] for n in range(5)]
    below = [sides_ref[5 + n] for n in range(5)]
    pulled = {}
    for n, cy in enumerate((-1, 0, 1)):
        equilibrium, source = (parts_ref[n], parts_ref[3 + n])
        right = jnp.where(has_right, jnp.where(upper, first_ref[n], second_ref[n]), 0.0)
        left = jnp.where(has_left, jnp.where(upper, second_ref[n], first_ref[n]), 0.0)
        moved = {
            0: (equilibrium, source),
            1: (jnp.where(first_half, half(equilibrium), half(right)), jnp.where(first_half, half(source), right)),
            -1: (jnp.where(first_half, left, half(equilibrium)), jnp.where(first_half, half(left), half(source))),
        }
        for c in DIRECTIONS:
            if c[1] != cy:
                continue
            shifted, added = moved[c[0]]
            if cy == 0:
                base = stay_ref[{0: 0, 1: 3, -1: 6}[c[0]] + {0: 0, 1: 1, -1: 2}[c[2]]]
            else:
                side = above if cy > 0 else below
                base = side[{0: {0: 0, 1: 1, -1: 2}[c[2]], 1: 3, -1: 4}[c[0]]]
            pulled[c] = along(base + shifted + WEIGHTS[INDEX[c]] * added, c[2])
    pulled = {c: pulled[c] for c in DIRECTIONS}
    density = moment(pulled, [fixed_ref[3 + c] for c in range(3)])
    write_payload(payload_ref, density, slots_ref)
    for i, c in enumerate(DIRECTIONS):
        pulled_ref[i] = pulled[c]
    density_ref[0] = density


def last_kernel(returned_ref, pulled_ref, density_ref, fixed_ref, out_ref):
    total = total_of(returned_ref, 16)
    rate = fixed_ref[0]
    keep = fixed_ref[2]
    source = fixed_ref[1] * (total[0:8] + total[8:16])
    shared = keep * rate * density_ref[0]
    here = keep * (1.0 - rate)
    for i in range(len(DIRECTIONS)):
        value = here * pulled_ref[i] + shared + WEIGHTS[i] * source
        for x in range(2):
            for s in range(SPECIES):
                row = 4 * x + s
                out_ref[s, i, x] = value[row : row + 1]


def call(kernel, out_shape, in_specs, name, **rest):
    single = not isinstance(out_shape, (tuple, list))
    return pl.pallas_call(
        kernel,
        out_shape=out_shape,
        in_specs=in_specs,
        out_specs=VM if single else tuple(VM for _ in out_shape),
        name=name,
        compiler_params=pltpu.CompilerParams(vmem_limit_bytes=32 * 1024 * 1024),
        **rest,
    )


def swapped(value, axis, odd):
    count = lax.axis_size(axis)
    step = [(1 if (i % 2 == 0) != odd else -1) for i in range(count)]
    return lax.ppermute(value, axis, [(i, (i + step[i]) % count) for i in range(count)])


def body(adjoint, velocity, relaxation, uptake, fluid_mask, block_cells, owner_load, response):
    owners = lax.axis_size("work")
    matrices = response.reshape(response.shape[2:])
    speeds = velocity.transpose(0, 2, 1, 3)

    def outside(value):
        return pltpu.with_memory_space_constraint(value, pltpu.HBM)

    def both_ways(near, far, axis):
        return swapped(near, axis, True), swapped(far, axis, False)

    def owner(incoming, fetched, fold):
        return call(
            lambda *refs: owner_kernel(*refs, fold=fold),
            jax.ShapeDtypeStruct((owners, 32 if fold else 16, LANES), BF16),
            [VM, VM],
            "owner_fold" if fold else "owner",
            scratch_shapes=[
                pltpu.VMEM((owners, 32, 2 * LANES), BF16),
                pltpu.VMEM((owners, 32, LANES), F32),
                pltpu.VMEM((owners, 8, LANES), F32),
            ],
        )(incoming, fetched)

    def exchange(value):
        return lax.all_to_all(value, "work", split_axis=0, concat_axis=0, tiled=True)

    payload_shape = jax.ShapeDtypeStruct((owners, 16, LANES), BF16)
    middle, near, far, fixed = call(
        arrange_kernel,
        (tile(9), tile(5), tile(5), tile(6)),
        [HBM] * 5,
        "arrange",
        scratch_shapes=[
            pltpu.VMEM(adjoint.shape, F32),
            pltpu.VMEM(speeds.shape, BF16),
            pltpu.VMEM(fluid_mask.shape, jnp.int32),
            pltpu.SMEM(relaxation.shape, F32),
            pltpu.SMEM(uptake.shape, F32),
            pltpu.VMEM((5, 8, LANES), F32),
            pltpu.VMEM((5, 8, LANES), F32),
            pltpu.SemaphoreType.DMA((5,)),
        ],
    )(*map(outside, (adjoint, speeds, fluid_mask, relaxation, uptake)))
    first, second = both_ways(near, far, "space")
    slots = call(
        slots_kernel,
        tile(owners, rows=16),
        [HBM] * 2,
        "slots",
        scratch_shapes=[
            pltpu.VMEM(block_cells.shape, jnp.int32),
            pltpu.SMEM(owner_load.shape, jnp.int32),
            pltpu.SemaphoreType.DMA((2,)),
        ],
    )(*map(outside, (block_cells, owner_load)))
    fetched, sides = call(
        fetch_kernel,
        (pltpu.VMEM(matrices.shape, BF16), tile(6)),
        [HBM, VM],
        "fetch",
        scratch_shapes=[pltpu.SemaphoreType.DMA((CHUNKS,))],
    )(outside(matrices), middle)
    one, two = call(across_kernel, (tile(7), tile(7)), [VM] * 5, "across")(sides, near, far, first, second)
    one, two = both_ways(one, two, "work")
    stay, third, fourth, gain, payload = call(
        first_kernel, (tile(9), tile(5), tile(5), tile(4), payload_shape), [VM] * 9, "first"
    )(middle, near, far, first, second, one, two, fixed, slots)
    incoming = exchange(payload)
    third, fourth = both_ways(third, fourth, "work")
    returned = exchange(owner(incoming, fetched, True))
    parts, near, far = call(gather_kernel, (tile(6), tile(3), tile(3)), [VM] * 4, "gather")(
        returned, incoming, gain, fixed
    )
    first, second = both_ways(near, far, "space")
    fetched, sides = call(
        fetch_again_kernel,
        (pltpu.VMEM(matrices.shape, BF16), tile(10)),
        [HBM, VM, VM],
        "fetch_again",
        scratch_shapes=[pltpu.SemaphoreType.DMA((CHUNKS,))],
    )(outside(matrices), third, fourth)
    pulled, density, payload = call(
        second_kernel, (tile(19), tile(1), payload_shape), [VM] * 7, "second"
    )(stay, sides, parts, first, second, fixed, slots)
    returned = exchange(owner(exchange(payload), fetched, False))
    return call(last_kernel, jax.ShapeDtypeStruct(adjoint.shape, F32), [VM] * 4, "last")(
        returned, pulled, density, fixed
    )


def solution(mesh):
    placed = (
        P(None, None, "space", "work", None),
        P(None, "space", "work", None),
        P(),
        P(),
        P("space", "work", None),
        P("space", "work", None, None, None),
        P("space", "work", None),
        P("space", "work", None, None, None, None),
    )
    return jax.shard_map(
        body,
        mesh=mesh,
        in_specs=placed,
        out_specs=P(None, None, "space", "work", None),
        check_vma=False,
    )
```

```python
import jax
import jax.numpy as jnp
from jax import lax
from jax.experimental import pallas as pl
from jax.experimental.pallas import tpu as pltpu
from jax.sharding import PartitionSpec as P

DIRECTIONS = (
    (0, 0, 0),
    (1, 0, 0),
    (-1, 0, 0),
    (0, 1, 0),
    (0, -1, 0),
    (0, 0, 1),
    (0, 0, -1),
    (1, 1, 0),
    (-1, -1, 0),
    (1, -1, 0),
    (-1, 1, 0),
    (1, 0, 1),
    (-1, 0, -1),
    (1, 0, -1),
    (-1, 0, 1),
    (0, 1, 1),
    (0, -1, -1),
    (0, 1, -1),
    (0, -1, 1),
)
WEIGHTS = (1.0 / 3.0,) + (1.0 / 18.0,) * 6 + (1.0 / 36.0,) * 12
INDEX = {c: i for i, c in enumerate(DIRECTIONS)}

MIDDLE = ((0, 0, 0), (0, 0, 1), (0, 0, -1), (0, 1, 0), (0, 1, 1), (0, 1, -1), (0, -1, 0), (0, -1, 1), (0, -1, -1))
PLUS = ((1, 0, 0), (1, 0, 1), (1, 0, -1), (1, 1, 0), (1, -1, 0))
MINUS = ((-1, 0, 0), (-1, 0, 1), (-1, 0, -1), (-1, 1, 0), (-1, -1, 0))
PLACE = {c: n for n, c in enumerate(MIDDLE)}
PLACE.update({c: n for n, c in enumerate(PLUS)})
PLACE.update({c: n for n, c in enumerate(MINUS)})
SPECIES = 3
LANES = 128
F32 = jnp.float32
BF16 = jnp.bfloat16
CHUNKS = 4
GROUP = 4
SECTION_BITS = 6
SECTION = 1 << SECTION_BITS
SECTIONS = LANES // SECTION

VM = pl.BlockSpec(memory_space=pltpu.VMEM)
SM = pl.BlockSpec(memory_space=pltpu.SMEM)
HBM = pl.BlockSpec(memory_space=pltpu.HBM)


def tile(count, dtype=F32, rows=8):
    return jax.ShapeDtypeStruct((count, rows, LANES), dtype)


def rows_of(shape=(8, LANES)):
    return lax.broadcasted_iota(jnp.int32, shape, 0)


def half(value):
    return pltpu.roll(value, 4, 0)


def along(value, step):
    return pltpu.roll(value, (-step) % LANES, 1) if step else value


def per_species(ref):
    species = rows_of() % 4
    out = jnp.zeros((8, LANES), F32)
    for s in range(SPECIES):
        out = jnp.where(species == s, ref[s], out)
    return out


def moment(pulled, speeds):
    density = None
    for c, value in pulled.items():
        factor = 1.0
        drift = None
        for axis in range(3):
            if c[axis]:
                part = speeds[axis] if c[axis] > 0 else -speeds[axis]
                drift = part if drift is None else drift + part
        weight = WEIGHTS[INDEX[c]]
        term = value * weight if drift is None else value * (weight + (3.0 * weight) * drift)
        density = term if density is None else density + term
    return density


def edges():
    a = lax.axis_index("space")
    b = lax.axis_index("work")
    return (a < lax.axis_size("space") - 1, a > 0, b < lax.axis_size("work") - 1, b > 0)


def near_is_upper(axis):
    return lax.axis_index(axis) % 2 == 1


def arrange_kernel(
    field_hbm, velocity_hbm, mask_hbm, relaxation_hbm, uptake_hbm,
    middle_ref, near_ref, far_ref, fixed_ref,
    field_ref, velocity_ref, mask_ref, relaxation_ref, uptake_ref, plus_ref, minus_ref, done,
):
    pairs = (
        (field_hbm, field_ref),
        (velocity_hbm, velocity_ref),
        (mask_hbm, mask_ref),
        (relaxation_hbm, relaxation_ref),
        (uptake_hbm, uptake_ref),
    )
    copies = [pltpu.make_async_copy(source, target, done.at[n]) for n, (source, target) in enumerate(pairs)]
    for copy in copies:
        copy.start()
    for copy in copies:
        copy.wait()
    first_half = rows_of() < 4
    keep = [mask_ref[x].astype(F32) for x in range(2)]
    for group, ref in ((MIDDLE, middle_ref), (PLUS, plus_ref), (MINUS, minus_ref)):
        for n, c in enumerate(group):
            for x in range(2):
                for s in range(SPECIES):
                    row = 4 * x + s
                    ref[n, row : row + 1, :] = field_ref[s, INDEX[c], x]
                ref[n, 4 * x + 3 : 4 * x + 4, :] = keep[x]
    upper = near_is_upper("space")
    for n in range(5):
        plus, minus = (plus_ref[n], minus_ref[n])
        near_ref[n] = jnp.where(upper, minus, plus)
        far_ref[n] = jnp.where(upper, plus, minus)
    fixed_ref[0] = per_species(relaxation_ref)
    fixed_ref[1] = per_species(uptake_ref)
    fixed_ref[2] = jnp.where(first_half, keep[0], keep[1])
    for c in range(3):
        speeds = velocity_ref[c, 0].astype(F32)
        fixed_ref[3 + c] = jnp.where(first_half, speeds[0:1], speeds[1:2])


def start_fetch(response_hbm, response_ref, done):
    parts = done.shape[0]
    each = response_hbm.shape[0] // parts
    copies = [
        pltpu.make_async_copy(
            response_hbm.at[pl.ds(n * each, each)], response_ref.at[pl.ds(n * each, each)], done.at[n]
        )
        for n in range(parts)
    ]
    for copy in copies:
        copy.start()
    return copies


def fetch_kernel(response_hbm, middle_ref, response_ref, sides_ref, done):
    copies = start_fetch(response_hbm, response_ref, done)
    sides_ref[...] = middle_ref[3:9]
    for copy in copies:
        copy.wait()


def fetch_again_kernel(response_hbm, third_ref, fourth_ref, response_ref, sides_ref, done):
    copies = start_fetch(response_hbm, response_ref, done)
    _, _, has_above, has_below = edges()
    upper_row = near_is_upper("work")
    for n in range(5):
        third, fourth = (third_ref[n], fourth_ref[n])
        sides_ref[n] = jnp.where(has_above, jnp.where(upper_row, third, fourth), 0.0)
        sides_ref[5 + n] = jnp.where(has_below, jnp.where(upper_row, fourth, third), 0.0)
    for copy in copies:
        copy.wait()


def slots_kernel(cells_hbm, load_hbm, slots_ref, cells_ref, load_ref, done):
    pairs = ((cells_hbm, cells_ref), (load_hbm, load_ref))
    copies = [pltpu.make_async_copy(source, target, done.at[n]) for n, (source, target) in enumerate(pairs)]
    for copy in copies:
        copy.start()
    for copy in copies:
        copy.wait()
    rows = rows_of()
    for q in range(slots_ref.shape[0]):
        load = load_ref[0, 0, q]
        cells = cells_ref[0, 0, q].astype(F32)
        live = [jnp.where(k < load, cells[k : k + 1], -1.0) for k in range(4)]
        for n in range(2):
            slots_ref[q, 8 * n : 8 * n + 8, :] = jnp.where(
                rows == 3, live[2 * n], jnp.where(rows == 7, live[2 * n + 1], 0.0)
            )


def across_kernel(sides_ref, near_ref, far_ref, first_ref, second_ref, one_ref, two_ref):
    has_right, has_left, _, _ = edges()
    upper = near_is_upper("space")
    upper_row = near_is_upper("work")
    pieces = {}
    for sign in (1, -1):
        p, m = (PLACE[(1, sign, 0)], PLACE[(-1, sign, 0)])
        pieces[sign] = [sides_ref[PLACE[(0, sign, cz)] - 3] for cz in (0, 1, -1)] + [
            jnp.where(upper, far_ref[p], near_ref[p]),
            jnp.where(has_right, jnp.where(upper, first_ref[p], second_ref[p]), 0.0),
            jnp.where(upper, near_ref[m], far_ref[m]),
            jnp.where(has_left, jnp.where(upper, second_ref[m], first_ref[m]), 0.0),
        ]
    for n in range(7):
        one_ref[n] = jnp.where(upper_row, pieces[-1][n], pieces[1][n])
        two_ref[n] = jnp.where(upper_row, pieces[1][n], pieces[-1][n])


def write_payload(payload_ref, density, slots_ref):
    live = rows_of() % 4 < SPECIES
    high = density.astype(BF16).astype(F32)
    both = jnp.concatenate([jnp.where(live, high, 0.0), jnp.where(live, density - high, 0.0)], axis=0)
    for q in range(payload_ref.shape[0]):
        payload_ref[q] = (both + slots_ref[q]).astype(BF16)


def first_kernel(
    middle_ref, near_ref, far_ref, first_ref, second_ref, one_ref, two_ref, fixed_ref, slots_ref,
    stay_ref, third_ref, fourth_ref, gain_ref, payload_ref,
):
    has_right, has_left, has_above, has_below = edges()
    upper = near_is_upper("space")
    upper_row = near_is_upper("work")
    first_half = rows_of() < 4
    rate = fixed_ref[0]
    keep = fixed_ref[2]
    plus = [jnp.where(upper, far_ref[n], near_ref[n]) for n in range(3)]
    minus = [jnp.where(upper, near_ref[n], far_ref[n]) for n in range(3)]
    right = [jnp.where(has_right, jnp.where(upper, first_ref[n], second_ref[n]), 0.0) for n in range(3)]
    left = [jnp.where(has_left, jnp.where(upper, second_ref[n], first_ref[n]), 0.0) for n in range(3)]
    above = [jnp.where(has_above, jnp.where(upper_row, one_ref[n], two_ref[n]), 0.0) for n in range(7)]
    below = [jnp.where(has_below, jnp.where(upper_row, two_ref[n], one_ref[n]), 0.0) for n in range(7)]
    pulled = {}
    for n, cz in enumerate((0, 1, -1)):
        pulled[(0, 0, cz)] = along(middle_ref[PLACE[(0, 0, cz)]], cz)
        pulled[(1, 0, cz)] = along(jnp.where(first_half, half(plus[n]), half(right[n])), cz)
        pulled[(-1, 0, cz)] = along(jnp.where(first_half, half(left[n]), half(minus[n])), cz)
    for sign, side in ((1, above), (-1, below)):
        for n, cz in enumerate((0, 1, -1)):
            pulled[(0, sign, cz)] = along(side[n], cz)
        pulled[(1, sign, 0)] = jnp.where(first_half, half(side[3]), half(side[4]))
        pulled[(-1, sign, 0)] = jnp.where(first_half, half(side[6]), half(side[5]))
    pulled = {c: pulled[c] for c in DIRECTIONS}
    density = moment(pulled, [fixed_ref[3 + c] for c in range(3)])
    write_payload(payload_ref, density, slots_ref)

    kept = 1.0 - rate
    right_mask = jnp.where(first_half, keep[4:5], right[0][3:4])
    left_mask = jnp.where(first_half, left[0][7:8], keep[0:1])
    here, to_right, to_left = (keep * kept, right_mask * kept, left_mask * kept)
    for n, cz in enumerate((0, 1, -1)):
        stay_ref[n] = here * pulled[(0, 0, cz)]
        stay_ref[3 + n] = to_right * along(right[n], cz)
        stay_ref[6 + n] = to_left * along(left[n], cz)
    sends = {}
    for sign, side in ((1, above), (-1, below)):
        sends[sign] = [here * pulled[(0, sign, cz)] for cz in (0, 1, -1)] + [to_right * side[4], to_left * side[6]]
    for n in range(5):
        third_ref[n] = jnp.where(upper_row, sends[-1][n], sends[1][n])
        fourth_ref[n] = jnp.where(upper_row, sends[1][n], sends[-1][n])
    gain_ref[0] = jnp.where(first_half, below[0][3:4], below[0][7:8]) * rate
    gain_ref[1] = keep * rate
    gain_ref[2] = jnp.where(first_half, above[0][3:4], above[0][7:8]) * rate
    gain_ref[3] = density


def owner_kernel(incoming_ref, density_ref, matrices_ref, out_ref, picked_ref, reply_ref, sums_ref, *, fold):
    count = incoming_ref.shape[0]
    column = jnp.where(rows_of() < 4, 0, 1)
    cell_rows = lax.broadcasted_iota(jnp.int32, (SECTION, LANES), 0)
    contract = (((1,), (1,)), ((), ()))
    zero = jnp.zeros((8, LANES), F32)
    slot_rows = (3, 7, 11, 15)
    def pick(b):
        tiles = incoming_ref[b].astype(F32)
        if fold:
            top = tiles[0:8]
        else:
            pair = density_ref[16 * (b // 2) : 16 * (b // 2) + 16, :].astype(F32)
            top = pair[0:8] if b % 2 == 0 else pair[8:16]
        picked = []
        for row in slot_rows:
            cell = jnp.broadcast_to(tiles[row : row + 1].astype(jnp.int32), (8, LANES))
            found = jnp.take_along_axis(top, cell & (LANES - 1), axis=1, mode="promise_in_bounds")
            picked.append(jnp.where((cell >> 7) == column, found, half(found)))
        upper = jnp.concatenate([picked[0], zero, picked[2], zero], axis=0)
        lower = jnp.concatenate([zero, picked[1], zero, picked[3]], axis=0)
        picked_ref[b] = jnp.concatenate([upper, lower], axis=1).astype(BF16)

    def respond(b):
        top = jnp.concatenate([matrices_ref[b, 0], matrices_ref[b, 1]], axis=1)
        bottom = jnp.concatenate([matrices_ref[b, 2], matrices_ref[b, 3]], axis=1)
        grid = jnp.concatenate([top, bottom], axis=0)
        reply = lax.dot_general(picked_ref[b], grid, contract, preferred_element_type=F32)
        reply_ref[b] = jnp.concatenate([reply[0:16, 0:LANES], reply[16:32, LANES:]], axis=0)

    def spread(b):
        tiles = incoming_ref[b].astype(F32)
        lefts = []
        rights = []
        for k, row in enumerate(slot_rows):
            cell = tiles[row : row + 1].astype(jnp.int32)
            section = jnp.broadcast_to(cell >> SECTION_BITS, (8, LANES))
            reply = reply_ref[b, 8 * k : 8 * k + 8, :]
            parts = [jnp.where(section == column * SECTIONS + m, reply, 0.0) for m in range(SECTIONS)]
            highs = [part.astype(BF16).astype(F32) for part in parts]
            lows = [part - high for part, high in zip(parts, highs)]
            lefts.append(jnp.concatenate(highs + lows, axis=0).astype(BF16))
            rights.append(jnp.where(cell_rows == (cell & (SECTION - 1)), 1.0, 0.0).astype(BF16))
        both = lax.dot_general(
            jnp.concatenate(lefts, axis=1), jnp.concatenate(rights, axis=1), contract, preferred_element_type=F32
        )
        sums = [
            both[8 * m : 8 * m + 8] + both[8 * (SECTIONS + m) : 8 * (SECTIONS + m) + 8] for m in range(SECTIONS)
        ]
        total = jnp.concatenate(sums, axis=1)
        sums_ref[b] = total
        if not fold:
            high = total.astype(BF16).astype(F32)
            out_ref[b, 0:16, :] = jnp.concatenate([high, total - high], axis=0).astype(BF16)

    stages = (pick, respond, spread)
    groups = count // GROUP
    for turn in range(groups + len(stages) - 1):
        for lag, stage in enumerate(stages):
            if 0 <= turn - lag < groups:
                for b in range((turn - lag) * GROUP, (turn - lag + 1) * GROUP):
                    stage(b)
    if fold:
        rows = rows_of()
        for pair in range(count // 2):
            packed = []
            for b in (2 * pair, 2 * pair + 1):
                total = sums_ref[b]
                high = total.astype(BF16).astype(F32)
                before = sums_ref[b - 1] if b > 0 else zero
                after = sums_ref[b + 1] if b < count - 1 else zero
                for value, third, seventh in ((high, 0, 1), (total - high, 2, 4), (before, 5, 6)):
                    value = jnp.where(rows == 3, after[third : third + 1], value)
                    packed.append(jnp.where(rows == 7, after[seventh : seventh + 1], value))
            out_ref[48 * pair : 48 * pair + 48, :] = jnp.concatenate(packed, axis=0).astype(BF16)


def total_of(returned_ref, rows):
    total = returned_ref[0, 0:rows, :].astype(F32)
    for q in range(1, returned_ref.shape[0]):
        total = total + returned_ref[q, 0:rows, :].astype(F32)
    return total


def gather_kernel(returned_ref, incoming_ref, gain_ref, fixed_ref, parts_ref, near_ref, far_ref):
    first_half = rows_of() < 4
    factor = fixed_ref[1]
    total = returned_ref[0:48, :].astype(F32)
    for pair in range(1, returned_ref.shape[0] // 48):
        total = total + returned_ref[48 * pair : 48 * pair + 48, :].astype(F32)
    total = total[0:24] + total[24:48]
    ends = [total[row : row + 1] for row in (3, 7, 11, 15, 19, 23)]
    after = jnp.concatenate(ends[0:3] + ends[0:1] + ends[3:6] + ends[0:1], axis=0)
    sources = (total[16:24], total[0:8] + total[8:16], after)
    b = lax.axis_index("work")
    last = lax.axis_size("work") - 1
    upper = near_is_upper("space")
    for n, source in enumerate(sources):
        source = factor * source
        if n == 1:
            density = gain_ref[3]
        else:
            tiles = incoming_ref[jnp.clip(b + n - 1, 0, last)].astype(F32)
            density = tiles[0:8] + tiles[8:16]
        equilibrium = gain_ref[n] * density
        parts_ref[n] = equilibrium
        parts_ref[3 + n] = source
        to_lower = jnp.where(first_half, equilibrium, half(source))
        to_upper = jnp.where(first_half, half(equilibrium), source)
        near_ref[n] = jnp.where(upper, to_upper, to_lower)
        far_ref[n] = jnp.where(upper, to_lower, to_upper)


def second_kernel(
    stay_ref, sides_ref, parts_ref, first_ref, second_ref, fixed_ref,
    pulled_ref, density_ref, payload_ref,
):
    has_right, has_left, _, _ = edges()
    upper = near_is_upper("space")
    first_half = rows_of() < 4
    above = [sides_ref[n] for n in range(5)]
    below = [sides_ref[5 + n] for n in range(5)]
    pulled = {}
    for n, cy in enumerate((-1, 0, 1)):
        equilibrium, source = (parts_ref[n], parts_ref[3 + n])
        right = jnp.where(has_right, jnp.where(upper, first_ref[n], second_ref[n]), 0.0)
        left = jnp.where(has_left, jnp.where(upper, second_ref[n], first_ref[n]), 0.0)
        moved = {
            0: (equilibrium, source),
            1: (jnp.where(first_half, half(equilibrium), half(right)), jnp.where(first_half, half(source), right)),
            -1: (jnp.where(first_half, left, half(equilibrium)), jnp.where(first_half, half(left), half(source))),
        }
        for c in DIRECTIONS:
            if c[1] != cy:
                continue
            shifted, added = moved[c[0]]
            if cy == 0:
                base = stay_ref[{0: 0, 1: 3, -1: 6}[c[0]] + {0: 0, 1: 1, -1: 2}[c[2]]]
            else:
                side = above if cy > 0 else below
                base = side[{0: {0: 0, 1: 1, -1: 2}[c[2]], 1: 3, -1: 4}[c[0]]]
            pulled[c] = along(base + shifted + WEIGHTS[INDEX[c]] * added, c[2])
    pulled = {c: pulled[c] for c in DIRECTIONS}
    density = moment(pulled, [fixed_ref[3 + c] for c in range(3)])
    twice = jnp.concatenate([density, density], axis=0).astype(BF16)
    for pair in range(payload_ref.shape[0] // 16):
        payload_ref[16 * pair : 16 * pair + 16, :] = twice
    for i, c in enumerate(DIRECTIONS):
        pulled_ref[i] = pulled[c]
    density_ref[0] = density


def last_kernel(returned_ref, pulled_ref, density_ref, fixed_ref, out_ref):
    total = total_of(returned_ref, 16)
    rate = fixed_ref[0]
    keep = fixed_ref[2]
    source = fixed_ref[1] * (total[0:8] + total[8:16])
    shared = keep * rate * density_ref[0]
    here = keep * (1.0 - rate)
    for i in range(len(DIRECTIONS)):
        value = here * pulled_ref[i] + shared + WEIGHTS[i] * source
        for x in range(2):
            for s in range(SPECIES):
                row = 4 * x + s
                out_ref[s, i, x] = value[row : row + 1]


def call(kernel, out_shape, in_specs, name, **rest):
    single = not isinstance(out_shape, (tuple, list))
    return pl.pallas_call(
        kernel,
        out_shape=out_shape,
        in_specs=in_specs,
        out_specs=VM if single else tuple(VM for _ in out_shape),
        name=name,
        compiler_params=pltpu.CompilerParams(vmem_limit_bytes=32 * 1024 * 1024),
        **rest,
    )


def swapped(value, axis, odd):
    count = lax.axis_size(axis)
    step = [(1 if (i % 2 == 0) != odd else -1) for i in range(count)]
    return lax.ppermute(value, axis, [(i, (i + step[i]) % count) for i in range(count)])


def body(adjoint, velocity, relaxation, uptake, fluid_mask, block_cells, owner_load, response):
    owners = lax.axis_size("work")
    matrices = response.reshape(response.shape[2:])
    speeds = velocity.transpose(0, 2, 1, 3)

    def outside(value):
        return pltpu.with_memory_space_constraint(value, pltpu.HBM)

    def both_ways(near, far, axis):
        return swapped(near, axis, True), swapped(far, axis, False)

    def owner(incoming, densities, fetched, fold):
        return call(
            lambda *refs: owner_kernel(*refs, fold=fold),
            jax.ShapeDtypeStruct((owners * 24, LANES) if fold else (owners, 16, LANES), BF16),
            [VM, VM, VM],
            "owner_fold" if fold else "owner",
            scratch_shapes=[
                pltpu.VMEM((owners, 32, 2 * LANES), BF16),
                pltpu.VMEM((owners, 32, LANES), F32),
                pltpu.VMEM((owners, 8, LANES), F32),
            ],
        )(incoming, densities, fetched)

    def exchange(value):
        return lax.all_to_all(value, "work", split_axis=0, concat_axis=0, tiled=True)

    payload_shape = jax.ShapeDtypeStruct((owners, 16, LANES), BF16)
    middle, near, far, fixed = call(
        arrange_kernel,
        (tile(9), tile(5), tile(5), tile(6)),
        [HBM] * 5,
        "arrange",
        scratch_shapes=[
            pltpu.VMEM(adjoint.shape, F32),
            pltpu.VMEM(speeds.shape, BF16),
            pltpu.VMEM(fluid_mask.shape, jnp.int32),
            pltpu.SMEM(relaxation.shape, F32),
            pltpu.SMEM(uptake.shape, F32),
            pltpu.VMEM((5, 8, LANES), F32),
            pltpu.VMEM((5, 8, LANES), F32),
            pltpu.SemaphoreType.DMA((5,)),
        ],
    )(*map(outside, (adjoint, speeds, fluid_mask, relaxation, uptake)))
    first, second = both_ways(near, far, "space")
    slots = call(
        slots_kernel,
        tile(owners, rows=16),
        [HBM] * 2,
        "slots",
        scratch_shapes=[
            pltpu.VMEM(block_cells.shape, jnp.int32),
            pltpu.SMEM(owner_load.shape, jnp.int32),
            pltpu.SemaphoreType.DMA((2,)),
        ],
    )(*map(outside, (block_cells, owner_load)))
    fetched, sides = call(
        fetch_kernel,
        (pltpu.VMEM(matrices.shape, BF16), tile(6)),
        [HBM, VM],
        "fetch",
        scratch_shapes=[pltpu.SemaphoreType.DMA((CHUNKS,))],
    )(outside(matrices), middle)
    one, two = call(across_kernel, (tile(7), tile(7)), [VM] * 5, "across")(sides, near, far, first, second)
    one, two = both_ways(one, two, "work")
    stay, third, fourth, gain, payload = call(
        first_kernel, (tile(9), tile(5), tile(5), tile(4), payload_shape), [VM] * 9, "first"
    )(middle, near, far, first, second, one, two, fixed, slots)
    incoming = exchange(payload)
    third, fourth = both_ways(third, fourth, "work")
    returned = owner(incoming, payload, fetched, True).reshape(owners, 24, LANES)
    returned = exchange(returned).reshape(-1, LANES)
    parts, near, far = call(gather_kernel, (tile(6), tile(3), tile(3)), [VM] * 4, "gather")(
        returned, incoming, gain, fixed
    )
    first, second = both_ways(near, far, "space")
    fetched, sides = call(
        fetch_again_kernel,
        (pltpu.VMEM(matrices.shape, BF16), tile(10)),
        [HBM, VM, VM],
        "fetch_again",
        scratch_shapes=[pltpu.SemaphoreType.DMA((CHUNKS,))],
    )(outside(matrices), third, fourth)
    pulled, density, payload = call(
        second_kernel, (tile(19), tile(1), jax.ShapeDtypeStruct((owners * 8, LANES), BF16)), [VM] * 6, "second"
    )(stay, sides, parts, first, second, fixed)
    densities = exchange(payload.reshape(owners, 8, LANES)).reshape(-1, LANES)
    returned = exchange(owner(incoming, densities, fetched, False))
    return call(last_kernel, jax.ShapeDtypeStruct(adjoint.shape, F32), [VM] * 4, "last")(
        returned, pulled, density, fixed
    )


def solution(mesh):
    placed = (
        P(None, None, "space", "work", None),
        P(None, "space", "work", None),
        P(),
        P(),
        P("space", "work", None),
        P("space", "work", None, None, None),
        P("space", "work", None),
        P("space", "work", None, None, None, None),
    )
    return jax.shard_map(
        body,
        mesh=mesh,
        in_specs=placed,
        out_specs=P(None, None, "space", "work", None),
        check_vma=False,
    )
```

```python
import jax
import jax.numpy as jnp
from jax import lax
from jax.experimental import pallas as pl
from jax.experimental.pallas import tpu as pltpu
from jax.sharding import PartitionSpec as P

DIRECTIONS = (
    (0, 0, 0),
    (1, 0, 0),
    (-1, 0, 0),
    (0, 1, 0),
    (0, -1, 0),
    (0, 0, 1),
    (0, 0, -1),
    (1, 1, 0),
    (-1, -1, 0),
    (1, -1, 0),
    (-1, 1, 0),
    (1, 0, 1),
    (-1, 0, -1),
    (1, 0, -1),
    (-1, 0, 1),
    (0, 1, 1),
    (0, -1, -1),
    (0, 1, -1),
    (0, -1, 1),
)
WEIGHTS = (1.0 / 3.0,) + (1.0 / 18.0,) * 6 + (1.0 / 36.0,) * 12
INDEX = {c: i for i, c in enumerate(DIRECTIONS)}

MIDDLE = ((0, 0, 0), (0, 0, 1), (0, 0, -1), (0, 1, 0), (0, 1, 1), (0, 1, -1), (0, -1, 0), (0, -1, 1), (0, -1, -1))
PLUS = ((1, 0, 0), (1, 0, 1), (1, 0, -1), (1, 1, 0), (1, -1, 0))
MINUS = ((-1, 0, 0), (-1, 0, 1), (-1, 0, -1), (-1, 1, 0), (-1, -1, 0))
PLACE = {c: n for n, c in enumerate(MIDDLE)}
PLACE.update({c: n for n, c in enumerate(PLUS)})
PLACE.update({c: n for n, c in enumerate(MINUS)})
SPECIES = 3
LANES = 128
F32 = jnp.float32
BF16 = jnp.bfloat16
CHUNKS = 4
GROUP = 4
SECTION_BITS = 6
SECTION = 1 << SECTION_BITS
SECTIONS = LANES // SECTION

VM = pl.BlockSpec(memory_space=pltpu.VMEM)
SM = pl.BlockSpec(memory_space=pltpu.SMEM)
HBM = pl.BlockSpec(memory_space=pltpu.HBM)


def tile(count, dtype=F32, rows=8):
    return jax.ShapeDtypeStruct((count, rows, LANES), dtype)


def rows_of(shape=(8, LANES)):
    return lax.broadcasted_iota(jnp.int32, shape, 0)


def half(value):
    return pltpu.roll(value, 4, 0)


def along(value, step):
    return pltpu.roll(value, (-step) % LANES, 1) if step else value


def per_species(ref):
    species = rows_of() % 4
    out = jnp.zeros((8, LANES), F32)
    for s in range(SPECIES):
        out = jnp.where(species == s, ref[s], out)
    return out


def moment(pulled, speeds):
    density = None
    for c, value in pulled.items():
        factor = 1.0
        drift = None
        for axis in range(3):
            if c[axis]:
                part = speeds[axis] if c[axis] > 0 else -speeds[axis]
                drift = part if drift is None else drift + part
        weight = WEIGHTS[INDEX[c]]
        term = value * weight if drift is None else value * (weight + (3.0 * weight) * drift)
        density = term if density is None else density + term
    return density


def edges():
    a = lax.axis_index("space")
    b = lax.axis_index("work")
    return (a < lax.axis_size("space") - 1, a > 0, b < lax.axis_size("work") - 1, b > 0)


def near_is_upper(axis):
    return lax.axis_index(axis) % 2 == 1


def arrange_kernel(
    field_hbm, velocity_hbm, mask_hbm, relaxation_hbm, uptake_hbm,
    middle_ref, near_ref, far_ref, fixed_ref,
    field_ref, velocity_ref, mask_ref, relaxation_ref, uptake_ref, plus_ref, minus_ref, done,
):
    pairs = (
        (field_hbm, field_ref),
        (velocity_hbm, velocity_ref),
        (mask_hbm, mask_ref),
        (relaxation_hbm, relaxation_ref),
        (uptake_hbm, uptake_ref),
    )
    copies = [pltpu.make_async_copy(source, target, done.at[n]) for n, (source, target) in enumerate(pairs)]
    for copy in copies:
        copy.start()
    for copy in copies:
        copy.wait()
    first_half = rows_of() < 4
    keep = [mask_ref[x].astype(F32) for x in range(2)]
    for group, ref in ((MIDDLE, middle_ref), (PLUS, plus_ref), (MINUS, minus_ref)):
        for n, c in enumerate(group):
            for x in range(2):
                for s in range(SPECIES):
                    row = 4 * x + s
                    ref[n, row : row + 1, :] = field_ref[s, INDEX[c], x]
                ref[n, 4 * x + 3 : 4 * x + 4, :] = keep[x]
    upper = near_is_upper("space")
    for n in range(5):
        plus, minus = (plus_ref[n], minus_ref[n])
        near_ref[n] = jnp.where(upper, minus, plus)
        far_ref[n] = jnp.where(upper, plus, minus)
    fixed_ref[0] = per_species(relaxation_ref)
    fixed_ref[1] = per_species(uptake_ref)
    fixed_ref[2] = jnp.where(first_half, keep[0], keep[1])
    for c in range(3):
        speeds = velocity_ref[c, 0].astype(F32)
        fixed_ref[3 + c] = jnp.where(first_half, speeds[0:1], speeds[1:2])


def start_fetch(response_hbm, response_ref, done):
    parts = done.shape[0]
    each = response_hbm.shape[0] // parts
    copies = [
        pltpu.make_async_copy(
            response_hbm.at[pl.ds(n * each, each)], response_ref.at[pl.ds(n * each, each)], done.at[n]
        )
        for n in range(parts)
    ]
    for copy in copies:
        copy.start()
    return copies


def fetch_kernel(response_hbm, middle_ref, response_ref, sides_ref, done):
    copies = start_fetch(response_hbm, response_ref, done)
    sides_ref[...] = middle_ref[3:9]
    for copy in copies:
        copy.wait()


def fetch_again_kernel(response_hbm, third_ref, fourth_ref, response_ref, sides_ref, done):
    copies = start_fetch(response_hbm, response_ref, done)
    _, _, has_above, has_below = edges()
    upper_row = near_is_upper("work")
    for n in range(5):
        third, fourth = (third_ref[n], fourth_ref[n])
        sides_ref[n] = jnp.where(has_above, jnp.where(upper_row, third, fourth), 0.0)
        sides_ref[5 + n] = jnp.where(has_below, jnp.where(upper_row, fourth, third), 0.0)
    for copy in copies:
        copy.wait()


def slots_kernel(cells_hbm, load_hbm, slots_ref, cells_ref, load_ref, done):
    pairs = ((cells_hbm, cells_ref), (load_hbm, load_ref))
    copies = [pltpu.make_async_copy(source, target, done.at[n]) for n, (source, target) in enumerate(pairs)]
    for copy in copies:
        copy.start()
    for copy in copies:
        copy.wait()
    rows = rows_of()
    for q in range(slots_ref.shape[0]):
        load = load_ref[0, 0, q]
        cells = cells_ref[0, 0, q].astype(F32)
        live = [jnp.where(k < load, cells[k : k + 1], -1.0) for k in range(4)]
        for n in range(2):
            slots_ref[q, 8 * n : 8 * n + 8, :] = jnp.where(
                rows == 3, live[2 * n], jnp.where(rows == 7, live[2 * n + 1], 0.0)
            )


def across_kernel(sides_ref, near_ref, far_ref, first_ref, second_ref, one_ref, two_ref):
    has_right, has_left, _, _ = edges()
    upper = near_is_upper("space")
    upper_row = near_is_upper("work")
    pieces = {}
    for sign in (1, -1):
        p, m = (PLACE[(1, sign, 0)], PLACE[(-1, sign, 0)])
        pieces[sign] = [sides_ref[PLACE[(0, sign, cz)] - 3] for cz in (0, 1, -1)] + [
            jnp.where(upper, far_ref[p], near_ref[p]),
            jnp.where(has_right, jnp.where(upper, first_ref[p], second_ref[p]), 0.0),
            jnp.where(upper, near_ref[m], far_ref[m]),
            jnp.where(has_left, jnp.where(upper, second_ref[m], first_ref[m]), 0.0),
        ]
    for n in range(7):
        one_ref[n] = jnp.where(upper_row, pieces[-1][n], pieces[1][n])
        two_ref[n] = jnp.where(upper_row, pieces[1][n], pieces[-1][n])


def write_payload(payload_ref, density, slots_ref):
    live = rows_of() % 4 < SPECIES
    high = density.astype(BF16).astype(F32)
    both = jnp.concatenate([jnp.where(live, high, 0.0), jnp.where(live, density - high, 0.0)], axis=0)
    for q in range(payload_ref.shape[0]):
        payload_ref[q] = (both + slots_ref[q]).astype(BF16)


def first_kernel(
    middle_ref, near_ref, far_ref, first_ref, second_ref, one_ref, two_ref, fixed_ref, slots_ref,
    stay_ref, third_ref, fourth_ref, gain_ref, payload_ref,
):
    has_right, has_left, has_above, has_below = edges()
    upper = near_is_upper("space")
    upper_row = near_is_upper("work")
    first_half = rows_of() < 4
    rate = fixed_ref[0]
    keep = fixed_ref[2]
    plus = [jnp.where(upper, far_ref[n], near_ref[n]) for n in range(3)]
    minus = [jnp.where(upper, near_ref[n], far_ref[n]) for n in range(3)]
    right = [jnp.where(has_right, jnp.where(upper, first_ref[n], second_ref[n]), 0.0) for n in range(3)]
    left = [jnp.where(has_left, jnp.where(upper, second_ref[n], first_ref[n]), 0.0) for n in range(3)]
    above = [jnp.where(has_above, jnp.where(upper_row, one_ref[n], two_ref[n]), 0.0) for n in range(7)]
    below = [jnp.where(has_below, jnp.where(upper_row, two_ref[n], one_ref[n]), 0.0) for n in range(7)]
    pulled = {}
    for n, cz in enumerate((0, 1, -1)):
        pulled[(0, 0, cz)] = along(middle_ref[PLACE[(0, 0, cz)]], cz)
        pulled[(1, 0, cz)] = along(jnp.where(first_half, half(plus[n]), half(right[n])), cz)
        pulled[(-1, 0, cz)] = along(jnp.where(first_half, half(left[n]), half(minus[n])), cz)
    for sign, side in ((1, above), (-1, below)):
        for n, cz in enumerate((0, 1, -1)):
            pulled[(0, sign, cz)] = along(side[n], cz)
        pulled[(1, sign, 0)] = jnp.where(first_half, half(side[3]), half(side[4]))
        pulled[(-1, sign, 0)] = jnp.where(first_half, half(side[6]), half(side[5]))
    pulled = {c: pulled[c] for c in DIRECTIONS}
    density = moment(pulled, [fixed_ref[3 + c] for c in range(3)])
    write_payload(payload_ref, density, slots_ref)

    kept = 1.0 - rate
    right_mask = jnp.where(first_half, keep[4:5], right[0][3:4])
    left_mask = jnp.where(first_half, left[0][7:8], keep[0:1])
    here, to_right, to_left = (keep * kept, right_mask * kept, left_mask * kept)
    for n, cz in enumerate((0, 1, -1)):
        stay_ref[n] = here * pulled[(0, 0, cz)]
        stay_ref[3 + n] = to_right * along(right[n], cz)
        stay_ref[6 + n] = to_left * along(left[n], cz)
    sends = {}
    for sign, side in ((1, above), (-1, below)):
        sends[sign] = [here * pulled[(0, sign, cz)] for cz in (0, 1, -1)] + [to_right * side[4], to_left * side[6]]
    for n in range(5):
        third_ref[n] = jnp.where(upper_row, sends[-1][n], sends[1][n])
        fourth_ref[n] = jnp.where(upper_row, sends[1][n], sends[-1][n])
    gain_ref[0] = jnp.where(first_half, below[0][3:4], below[0][7:8]) * rate
    gain_ref[1] = keep * rate
    gain_ref[2] = jnp.where(first_half, above[0][3:4], above[0][7:8]) * rate
    gain_ref[3] = density


def owner_kernel(incoming_ref, density_ref, matrices_ref, out_ref, picked_ref, reply_ref, sums_ref, *, fold):
    count = incoming_ref.shape[0]
    column = jnp.where(rows_of() < 4, 0, 1)
    cell_rows = lax.broadcasted_iota(jnp.int32, (SECTION, LANES), 0)
    contract = (((1,), (1,)), ((), ()))
    zero = jnp.zeros((8, LANES), F32)
    slot_rows = (3, 7, 11, 15)
    def pick(b):
        tiles = incoming_ref[b].astype(F32)
        if fold:
            top = tiles[0:8]
        else:
            pair = density_ref[16 * (b // 2) : 16 * (b // 2) + 16, :].astype(F32)
            top = pair[0:8] if b % 2 == 0 else pair[8:16]
        picked = []
        for row in slot_rows:
            cell = jnp.broadcast_to(tiles[row : row + 1].astype(jnp.int32), (8, LANES))
            found = jnp.take_along_axis(top, cell & (LANES - 1), axis=1, mode="promise_in_bounds")
            picked.append(jnp.where((cell >> 7) == column, found, half(found)))
        upper = jnp.concatenate([picked[0], zero, picked[2], zero], axis=0)
        lower = jnp.concatenate([zero, picked[1], zero, picked[3]], axis=0)
        picked_ref[b] = jnp.concatenate([upper, lower], axis=1).astype(BF16)

    def respond(b):
        top = jnp.concatenate([matrices_ref[b, 0], matrices_ref[b, 1]], axis=1)
        bottom = jnp.concatenate([matrices_ref[b, 2], matrices_ref[b, 3]], axis=1)
        grid = jnp.concatenate([top, bottom], axis=0)
        reply = lax.dot_general(picked_ref[b], grid, contract, preferred_element_type=F32)
        reply_ref[b] = jnp.concatenate([reply[0:16, 0:LANES], reply[16:32, LANES:]], axis=0)

    def spread(b):
        tiles = incoming_ref[b].astype(F32)
        lefts = []
        rights = []
        for k, row in enumerate(slot_rows):
            cell = tiles[row : row + 1].astype(jnp.int32)
            section = jnp.broadcast_to(cell >> SECTION_BITS, (8, LANES))
            reply = reply_ref[b, 8 * k : 8 * k + 8, :]
            parts = [jnp.where(section == column * SECTIONS + m, reply, 0.0) for m in range(SECTIONS)]
            highs = [part.astype(BF16).astype(F32) for part in parts]
            lows = [part - high for part, high in zip(parts, highs)]
            lefts.append(jnp.concatenate(highs + lows, axis=0).astype(BF16))
            rights.append(jnp.where(cell_rows == (cell & (SECTION - 1)), 1.0, 0.0).astype(BF16))
        both = lax.dot_general(
            jnp.concatenate(lefts, axis=1), jnp.concatenate(rights, axis=1), contract, preferred_element_type=F32
        )
        sums = [
            both[8 * m : 8 * m + 8] + both[8 * (SECTIONS + m) : 8 * (SECTIONS + m) + 8] for m in range(SECTIONS)
        ]
        total = jnp.concatenate(sums, axis=1)
        sums_ref[b] = total
        if not fold:
            high = total.astype(BF16).astype(F32)
            out_ref[b, 0:16, :] = jnp.concatenate([high, total - high], axis=0).astype(BF16)

    stages = (pick, respond, spread)
    groups = count // GROUP
    for turn in range(groups + len(stages) - 1):
        for lag, stage in enumerate(stages):
            if 0 <= turn - lag < groups:
                for b in range((turn - lag) * GROUP, (turn - lag + 1) * GROUP):
                    stage(b)
    if fold:
        rows = rows_of()
        for pair in range(count // 2):
            packed = []
            for b in (2 * pair, 2 * pair + 1):
                total = sums_ref[b]
                high = total.astype(BF16).astype(F32)
                before = sums_ref[b - 1] if b > 0 else zero
                after = sums_ref[b + 1] if b < count - 1 else zero
                for value, third, seventh in ((high, 0, 1), (total - high, 2, 4), (before, 5, 6)):
                    value = jnp.where(rows == 3, after[third : third + 1], value)
                    packed.append(jnp.where(rows == 7, after[seventh : seventh + 1], value))
            out_ref[48 * pair : 48 * pair + 48, :] = jnp.concatenate(packed, axis=0).astype(BF16)


def total_of(returned_ref, rows):
    total = returned_ref[0, 0:rows, :].astype(F32)
    for q in range(1, returned_ref.shape[0]):
        total = total + returned_ref[q, 0:rows, :].astype(F32)
    return total


def gather_kernel(returned_ref, incoming_ref, gain_ref, fixed_ref, parts_ref, near_ref, far_ref):
    first_half = rows_of() < 4
    factor = fixed_ref[1]
    total = returned_ref[0:48, :].astype(F32)
    for pair in range(1, returned_ref.shape[0] // 48):
        total = total + returned_ref[48 * pair : 48 * pair + 48, :].astype(F32)
    total = total[0:24] + total[24:48]
    ends = [total[row : row + 1] for row in (3, 7, 11, 15, 19, 23)]
    after = jnp.concatenate(ends[0:3] + ends[0:1] + ends[3:6] + ends[0:1], axis=0)
    sources = (total[16:24], total[0:8] + total[8:16], after)
    b = lax.axis_index("work")
    last = lax.axis_size("work") - 1
    upper = near_is_upper("space")
    for n, source in enumerate(sources):
        source = factor * source
        if n == 1:
            density = gain_ref[3]
        else:
            tiles = incoming_ref[jnp.clip(b + n - 1, 0, last)].astype(F32)
            density = tiles[0:8] + tiles[8:16]
        equilibrium = gain_ref[n] * density
        parts_ref[n] = equilibrium
        parts_ref[3 + n] = source
        to_lower = jnp.where(first_half, equilibrium, half(source))
        to_upper = jnp.where(first_half, half(equilibrium), source)
        near_ref[n] = jnp.where(upper, to_upper, to_lower)
        far_ref[n] = jnp.where(upper, to_lower, to_upper)


def second_kernel(
    stay_ref, sides_ref, parts_ref, first_ref, second_ref, fixed_ref,
    pulled_ref, density_ref, payload_ref,
):
    has_right, has_left, _, _ = edges()
    upper = near_is_upper("space")
    first_half = rows_of() < 4
    above = [sides_ref[n] for n in range(5)]
    below = [sides_ref[5 + n] for n in range(5)]
    pulled = {}
    for n, cy in enumerate((-1, 0, 1)):
        equilibrium, source = (parts_ref[n], parts_ref[3 + n])
        right = jnp.where(has_right, jnp.where(upper, first_ref[n], second_ref[n]), 0.0)
        left = jnp.where(has_left, jnp.where(upper, second_ref[n], first_ref[n]), 0.0)
        moved = {
            0: (equilibrium, source),
            1: (jnp.where(first_half, half(equilibrium), half(right)), jnp.where(first_half, half(source), right)),
            -1: (jnp.where(first_half, left, half(equilibrium)), jnp.where(first_half, half(left), half(source))),
        }
        for c in DIRECTIONS:
            if c[1] != cy:
                continue
            shifted, added = moved[c[0]]
            if cy == 0:
                base = stay_ref[{0: 0, 1: 3, -1: 6}[c[0]] + {0: 0, 1: 1, -1: 2}[c[2]]]
            else:
                side = above if cy > 0 else below
                base = side[{0: {0: 0, 1: 1, -1: 2}[c[2]], 1: 3, -1: 4}[c[0]]]
            pulled[c] = along(base + shifted + WEIGHTS[INDEX[c]] * added, c[2])
    pulled = {c: pulled[c] for c in DIRECTIONS}
    density = moment(pulled, [fixed_ref[3 + c] for c in range(3)])
    twice = jnp.concatenate([density, density], axis=0).astype(BF16)
    for pair in range(payload_ref.shape[0] // 16):
        payload_ref[16 * pair : 16 * pair + 16, :] = twice
    for i, c in enumerate(DIRECTIONS):
        pulled_ref[i] = pulled[c]
    density_ref[0] = density


def last_kernel(returned_ref, pulled_ref, density_ref, fixed_ref, out_ref):
    total = total_of(returned_ref, 16)
    rate = fixed_ref[0]
    keep = fixed_ref[2]
    source = fixed_ref[1] * (total[0:8] + total[8:16])
    shared = keep * rate * density_ref[0]
    here = keep * (1.0 - rate)
    for i in range(len(DIRECTIONS)):
        value = here * pulled_ref[i] + shared + WEIGHTS[i] * source
        for x in range(2):
            for s in range(SPECIES):
                row = 4 * x + s
                out_ref[s, i, x] = value[row : row + 1]


def call(kernel, out_shape, in_specs, name, **rest):
    single = not isinstance(out_shape, (tuple, list))
    return pl.pallas_call(
        kernel,
        out_shape=out_shape,
        in_specs=in_specs,
        out_specs=VM if single else tuple(VM for _ in out_shape),
        name=name,
        compiler_params=pltpu.CompilerParams(vmem_limit_bytes=32 * 1024 * 1024),
        **rest,
    )


def swapped(value, axis, odd):
    columns, owners = (lax.axis_size("space"), lax.axis_size("work"))
    pairs = []
    for a in range(columns):
        for b in range(owners):
            at, count = (b, owners) if axis == "work" else (a, columns)
            to = at + (1 if (at % 2 == 0) != odd else -1)
            if 0 <= to < count:
                other = to * owners + b if axis == "space" else a * owners + to
            else:
                other = a * owners + (b ^ 1) if axis == "space" else (a ^ 1) * owners + b
            pairs.append((a * owners + b, other))
    return lax.ppermute(value, ("space", "work"), pairs)


def body(adjoint, velocity, relaxation, uptake, fluid_mask, block_cells, owner_load, response):
    owners = lax.axis_size("work")
    matrices = response.reshape(response.shape[2:])
    speeds = velocity.transpose(0, 2, 1, 3)

    def outside(value):
        return pltpu.with_memory_space_constraint(value, pltpu.HBM)

    def both_ways(near, far, axis):
        return swapped(near, axis, True), swapped(far, axis, False)

    def owner(incoming, densities, fetched, fold):
        return call(
            lambda *refs: owner_kernel(*refs, fold=fold),
            jax.ShapeDtypeStruct((owners * 24, LANES) if fold else (owners, 16, LANES), BF16),
            [VM, VM, VM],
            "owner_fold" if fold else "owner",
            scratch_shapes=[
                pltpu.VMEM((owners, 32, 2 * LANES), BF16),
                pltpu.VMEM((owners, 32, LANES), F32),
                pltpu.VMEM((owners, 8, LANES), F32),
            ],
        )(incoming, densities, fetched)

    def exchange(value):
        return lax.all_to_all(value, "work", split_axis=0, concat_axis=0, tiled=True)

    payload_shape = jax.ShapeDtypeStruct((owners, 16, LANES), BF16)
    middle, near, far, fixed = call(
        arrange_kernel,
        (tile(9), tile(5), tile(5), tile(6)),
        [HBM] * 5,
        "arrange",
        scratch_shapes=[
            pltpu.VMEM(adjoint.shape, F32),
            pltpu.VMEM(speeds.shape, BF16),
            pltpu.VMEM(fluid_mask.shape, jnp.int32),
            pltpu.SMEM(relaxation.shape, F32),
            pltpu.SMEM(uptake.shape, F32),
            pltpu.VMEM((5, 8, LANES), F32),
            pltpu.VMEM((5, 8, LANES), F32),
            pltpu.SemaphoreType.DMA((5,)),
        ],
    )(*map(outside, (adjoint, speeds, fluid_mask, relaxation, uptake)))
    first, second = both_ways(near, far, "space")
    slots = call(
        slots_kernel,
        tile(owners, rows=16),
        [HBM] * 2,
        "slots",
        scratch_shapes=[
            pltpu.VMEM(block_cells.shape, jnp.int32),
            pltpu.SMEM(owner_load.shape, jnp.int32),
            pltpu.SemaphoreType.DMA((2,)),
        ],
    )(*map(outside, (block_cells, owner_load)))
    fetched, sides = call(
        fetch_kernel,
        (pltpu.VMEM(matrices.shape, BF16), tile(6)),
        [HBM, VM],
        "fetch",
        scratch_shapes=[pltpu.SemaphoreType.DMA((CHUNKS,))],
    )(outside(matrices), middle)
    one, two = call(across_kernel, (tile(7), tile(7)), [VM] * 5, "across")(sides, near, far, first, second)
    one, two = both_ways(one, two, "work")
    stay, third, fourth, gain, payload = call(
        first_kernel, (tile(9), tile(5), tile(5), tile(4), payload_shape), [VM] * 9, "first"
    )(middle, near, far, first, second, one, two, fixed, slots)
    incoming = exchange(payload)
    third, fourth = both_ways(third, fourth, "work")
    returned = owner(incoming, payload, fetched, True).reshape(owners, 24, LANES)
    returned = exchange(returned).reshape(-1, LANES)
    parts, near, far = call(gather_kernel, (tile(6), tile(3), tile(3)), [VM] * 4, "gather")(
        returned, incoming, gain, fixed
    )
    first, second = both_ways(near, far, "space")
    fetched, sides = call(
        fetch_again_kernel,
        (pltpu.VMEM(matrices.shape, BF16), tile(10)),
        [HBM, VM, VM],
        "fetch_again",
        scratch_shapes=[pltpu.SemaphoreType.DMA((CHUNKS,))],
    )(outside(matrices), third, fourth)
    pulled, density, payload = call(
        second_kernel, (tile(19), tile(1), jax.ShapeDtypeStruct((owners * 8, LANES), BF16)), [VM] * 6, "second"
    )(stay, sides, parts, first, second, fixed)
    densities = exchange(payload.reshape(owners, 8, LANES)).reshape(-1, LANES)
    returned = exchange(owner(incoming, densities, fetched, False))
    return call(last_kernel, jax.ShapeDtypeStruct(adjoint.shape, F32), [VM] * 4, "last")(
        returned, pulled, density, fixed
    )


def solution(mesh):
    placed = (
        P(None, None, "space", "work", None),
        P(None, "space", "work", None),
        P(),
        P(),
        P("space", "work", None),
        P("space", "work", None, None, None),
        P("space", "work", None),
        P("space", "work", None, None, None, None),
    )
    return jax.shard_map(
        body,
        mesh=mesh,
        in_specs=placed,
        out_specs=P(None, None, "space", "work", None),
        check_vma=False,
    )
```

```python
import jax
import jax.numpy as jnp
from jax import lax
from jax.experimental import pallas as pl
from jax.experimental.pallas import tpu as pltpu
from jax.sharding import PartitionSpec as P

DIRECTIONS = (
    (0, 0, 0),
    (1, 0, 0),
    (-1, 0, 0),
    (0, 1, 0),
    (0, -1, 0),
    (0, 0, 1),
    (0, 0, -1),
    (1, 1, 0),
    (-1, -1, 0),
    (1, -1, 0),
    (-1, 1, 0),
    (1, 0, 1),
    (-1, 0, -1),
    (1, 0, -1),
    (-1, 0, 1),
    (0, 1, 1),
    (0, -1, -1),
    (0, 1, -1),
    (0, -1, 1),
)
WEIGHTS = (1.0 / 3.0,) + (1.0 / 18.0,) * 6 + (1.0 / 36.0,) * 12
INDEX = {c: i for i, c in enumerate(DIRECTIONS)}

MIDDLE = ((0, 0, 0), (0, 0, 1), (0, 0, -1), (0, 1, 0), (0, 1, 1), (0, 1, -1), (0, -1, 0), (0, -1, 1), (0, -1, -1))
PLUS = ((1, 0, 0), (1, 0, 1), (1, 0, -1), (1, 1, 0), (1, -1, 0))
MINUS = ((-1, 0, 0), (-1, 0, 1), (-1, 0, -1), (-1, 1, 0), (-1, -1, 0))
PLACE = {c: n for n, c in enumerate(MIDDLE)}
PLACE.update({c: n for n, c in enumerate(PLUS)})
PLACE.update({c: n for n, c in enumerate(MINUS)})
SPECIES = 3
LANES = 128
F32 = jnp.float32
BF16 = jnp.bfloat16
CHUNKS = 4
GROUP = 4
SECTION_BITS = 6
SECTION = 1 << SECTION_BITS
SECTIONS = LANES // SECTION

VM = pl.BlockSpec(memory_space=pltpu.VMEM)
SM = pl.BlockSpec(memory_space=pltpu.SMEM)
HBM = pl.BlockSpec(memory_space=pltpu.HBM)


def tile(count, dtype=F32, rows=8):
    return jax.ShapeDtypeStruct((count, rows, LANES), dtype)


def rows_of(shape=(8, LANES)):
    return lax.broadcasted_iota(jnp.int32, shape, 0)


def half(value):
    return pltpu.roll(value, 4, 0)


def along(value, step):
    return pltpu.roll(value, (-step) % LANES, 1) if step else value


def per_species(ref):
    species = rows_of() % 4
    out = jnp.zeros((8, LANES), F32)
    for s in range(SPECIES):
        out = jnp.where(species == s, ref[s], out)
    return out


def moment(pulled, speeds):
    density = None
    for c, value in pulled.items():
        factor = 1.0
        drift = None
        for axis in range(3):
            if c[axis]:
                part = speeds[axis] if c[axis] > 0 else -speeds[axis]
                drift = part if drift is None else drift + part
        weight = WEIGHTS[INDEX[c]]
        term = value * weight if drift is None else value * (weight + (3.0 * weight) * drift)
        density = term if density is None else density + term
    return density


def edges():
    a = lax.axis_index("space")
    b = lax.axis_index("work")
    return (a < lax.axis_size("space") - 1, a > 0, b < lax.axis_size("work") - 1, b > 0)


def near_is_upper(axis):
    return lax.axis_index(axis) % 2 == (1 if axis == "work" else 0)


def arrange_kernel(
    field_hbm, velocity_hbm, mask_hbm, relaxation_hbm, uptake_hbm,
    middle_ref, near_ref, far_ref, fixed_ref,
    field_ref, velocity_ref, mask_ref, relaxation_ref, uptake_ref, plus_ref, minus_ref, done,
):
    pairs = (
        (field_hbm, field_ref),
        (velocity_hbm, velocity_ref),
        (mask_hbm, mask_ref),
        (relaxation_hbm, relaxation_ref),
        (uptake_hbm, uptake_ref),
    )
    copies = [pltpu.make_async_copy(source, target, done.at[n]) for n, (source, target) in enumerate(pairs)]
    for copy in copies:
        copy.start()
    for copy in copies:
        copy.wait()
    first_half = rows_of() < 4
    keep = [mask_ref[x].astype(F32) for x in range(2)]
    for group, ref in ((MIDDLE, middle_ref), (PLUS, plus_ref), (MINUS, minus_ref)):
        for n, c in enumerate(group):
            for x in range(2):
                for s in range(SPECIES):
                    row = 4 * x + s
                    ref[n, row : row + 1, :] = field_ref[s, INDEX[c], x]
                ref[n, 4 * x + 3 : 4 * x + 4, :] = keep[x]
    upper = near_is_upper("space")
    for n in range(5):
        plus, minus = (plus_ref[n], minus_ref[n])
        near_ref[n] = jnp.where(upper, minus, plus)
        far_ref[n] = jnp.where(upper, plus, minus)
    fixed_ref[0] = per_species(relaxation_ref)
    fixed_ref[1] = per_species(uptake_ref)
    fixed_ref[2] = jnp.where(first_half, keep[0], keep[1])
    for c in range(3):
        speeds = velocity_ref[c, 0].astype(F32)
        fixed_ref[3 + c] = jnp.where(first_half, speeds[0:1], speeds[1:2])


def start_fetch(response_hbm, response_ref, done):
    parts = done.shape[0]
    each = response_hbm.shape[0] // parts
    copies = [
        pltpu.make_async_copy(
            response_hbm.at[pl.ds(n * each, each)], response_ref.at[pl.ds(n * each, each)], done.at[n]
        )
        for n in range(parts)
    ]
    for copy in copies:
        copy.start()
    return copies


def fetch_kernel(response_hbm, middle_ref, response_ref, own_ref, done):
    copies = start_fetch(response_hbm, response_ref, done)
    own_ref[...] = middle_ref[0:3]
    for copy in copies:
        copy.wait()


def fetch_again_kernel(response_hbm, third_ref, fourth_ref, response_ref, sides_ref, done):
    copies = start_fetch(response_hbm, response_ref, done)
    _, _, has_above, has_below = edges()
    upper_row = near_is_upper("work")
    for n in range(5):
        third, fourth = (third_ref[n], fourth_ref[n])
        sides_ref[n] = jnp.where(has_above, jnp.where(upper_row, third, fourth), 0.0)
        sides_ref[5 + n] = jnp.where(has_below, jnp.where(upper_row, fourth, third), 0.0)
    for copy in copies:
        copy.wait()


def slots_kernel(cells_hbm, load_hbm, middle_ref, slots_ref, sides_ref, cells_ref, load_ref, done):
    pairs = ((cells_hbm, cells_ref), (load_hbm, load_ref))
    copies = [pltpu.make_async_copy(source, target, done.at[n]) for n, (source, target) in enumerate(pairs)]
    for copy in copies:
        copy.start()
    sides_ref[...] = middle_ref[3:9]
    for copy in copies:
        copy.wait()
    rows = rows_of()
    for q in range(slots_ref.shape[0]):
        load = load_ref[0, 0, q]
        cells = cells_ref[0, 0, q].astype(F32)
        live = [jnp.where(k < load, cells[k : k + 1], -1.0) for k in range(4)]
        for n in range(2):
            slots_ref[q, 8 * n : 8 * n + 8, :] = jnp.where(
                rows == 3, live[2 * n], jnp.where(rows == 7, live[2 * n + 1], 0.0)
            )


def across_kernel(sides_ref, near_ref, far_ref, first_ref, second_ref, one_ref, two_ref):
    has_right, has_left, _, _ = edges()
    upper = near_is_upper("space")
    upper_row = near_is_upper("work")
    pieces = {}
    for sign in (1, -1):
        p, m = (PLACE[(1, sign, 0)], PLACE[(-1, sign, 0)])
        pieces[sign] = [sides_ref[PLACE[(0, sign, cz)] - 3] for cz in (0, 1, -1)] + [
            jnp.where(upper, far_ref[p], near_ref[p]),
            jnp.where(has_right, jnp.where(upper, first_ref[p], second_ref[p]), 0.0),
            jnp.where(upper, near_ref[m], far_ref[m]),
            jnp.where(has_left, jnp.where(upper, second_ref[m], first_ref[m]), 0.0),
        ]
    for n in range(7):
        one_ref[n] = jnp.where(upper_row, pieces[-1][n], pieces[1][n])
        two_ref[n] = jnp.where(upper_row, pieces[1][n], pieces[-1][n])


def write_payload(payload_ref, density, slots_ref):
    live = rows_of() % 4 < SPECIES
    high = density.astype(BF16).astype(F32)
    both = jnp.concatenate([jnp.where(live, high, 0.0), jnp.where(live, density - high, 0.0)], axis=0)
    for q in range(payload_ref.shape[0]):
        payload_ref[q] = (both + slots_ref[q]).astype(BF16)


def first_kernel(
    middle_ref, near_ref, far_ref, first_ref, second_ref, one_ref, two_ref, fixed_ref, slots_ref,
    stay_ref, third_ref, fourth_ref, gain_ref, payload_ref,
):
    has_right, has_left, has_above, has_below = edges()
    upper = near_is_upper("space")
    upper_row = near_is_upper("work")
    first_half = rows_of() < 4
    rate = fixed_ref[0]
    keep = fixed_ref[2]
    plus = [jnp.where(upper, far_ref[n], near_ref[n]) for n in range(3)]
    minus = [jnp.where(upper, near_ref[n], far_ref[n]) for n in range(3)]
    right = [jnp.where(has_right, jnp.where(upper, first_ref[n], second_ref[n]), 0.0) for n in range(3)]
    left = [jnp.where(has_left, jnp.where(upper, second_ref[n], first_ref[n]), 0.0) for n in range(3)]
    above = [jnp.where(has_above, jnp.where(upper_row, one_ref[n], two_ref[n]), 0.0) for n in range(7)]
    below = [jnp.where(has_below, jnp.where(upper_row, two_ref[n], one_ref[n]), 0.0) for n in range(7)]
    pulled = {}
    for n, cz in enumerate((0, 1, -1)):
        pulled[(0, 0, cz)] = along(middle_ref[PLACE[(0, 0, cz)]], cz)
        pulled[(1, 0, cz)] = along(jnp.where(first_half, half(plus[n]), half(right[n])), cz)
        pulled[(-1, 0, cz)] = along(jnp.where(first_half, half(left[n]), half(minus[n])), cz)
    for sign, side in ((1, above), (-1, below)):
        for n, cz in enumerate((0, 1, -1)):
            pulled[(0, sign, cz)] = along(side[n], cz)
        pulled[(1, sign, 0)] = jnp.where(first_half, half(side[3]), half(side[4]))
        pulled[(-1, sign, 0)] = jnp.where(first_half, half(side[6]), half(side[5]))
    pulled = {c: pulled[c] for c in DIRECTIONS}
    density = moment(pulled, [fixed_ref[3 + c] for c in range(3)])
    write_payload(payload_ref, density, slots_ref)

    kept = 1.0 - rate
    right_mask = jnp.where(first_half, keep[4:5], right[0][3:4])
    left_mask = jnp.where(first_half, left[0][7:8], keep[0:1])
    here, to_right, to_left = (keep * kept, right_mask * kept, left_mask * kept)
    for n, cz in enumerate((0, 1, -1)):
        stay_ref[n] = here * pulled[(0, 0, cz)]
        stay_ref[3 + n] = to_right * along(right[n], cz)
        stay_ref[6 + n] = to_left * along(left[n], cz)
    sends = {}
    for sign, side in ((1, above), (-1, below)):
        sends[sign] = [here * pulled[(0, sign, cz)] for cz in (0, 1, -1)] + [to_right * side[4], to_left * side[6]]
    for n in range(5):
        third_ref[n] = jnp.where(upper_row, sends[-1][n], sends[1][n])
        fourth_ref[n] = jnp.where(upper_row, sends[1][n], sends[-1][n])
    gain_ref[0] = jnp.where(first_half, below[0][3:4], below[0][7:8]) * rate
    gain_ref[1] = keep * rate
    gain_ref[2] = jnp.where(first_half, above[0][3:4], above[0][7:8]) * rate
    gain_ref[3] = density


def owner_kernel(incoming_ref, density_ref, matrices_ref, out_ref, picked_ref, reply_ref, sums_ref, *, fold):
    count = incoming_ref.shape[0]
    column = jnp.where(rows_of() < 4, 0, 1)
    cell_rows = lax.broadcasted_iota(jnp.int32, (SECTION, LANES), 0)
    contract = (((1,), (1,)), ((), ()))
    zero = jnp.zeros((8, LANES), F32)
    slot_rows = (3, 7, 11, 15)
    def pick(b):
        tiles = incoming_ref[b].astype(F32)
        if fold:
            top = tiles[0:8]
        else:
            pair = density_ref[16 * (b // 2) : 16 * (b // 2) + 16, :].astype(F32)
            top = pair[0:8] if b % 2 == 0 else pair[8:16]
        picked = []
        for row in slot_rows:
            cell = jnp.broadcast_to(tiles[row : row + 1].astype(jnp.int32), (8, LANES))
            found = jnp.take_along_axis(top, cell & (LANES - 1), axis=1, mode="promise_in_bounds")
            picked.append(jnp.where((cell >> 7) == column, found, half(found)))
        upper = jnp.concatenate([picked[0], zero, picked[2], zero], axis=0)
        lower = jnp.concatenate([zero, picked[1], zero, picked[3]], axis=0)
        picked_ref[b] = jnp.concatenate([upper, lower], axis=1).astype(BF16)

    def respond(b):
        top = jnp.concatenate([matrices_ref[b, 0], matrices_ref[b, 1]], axis=1)
        bottom = jnp.concatenate([matrices_ref[b, 2], matrices_ref[b, 3]], axis=1)
        grid = jnp.concatenate([top, bottom], axis=0)
        reply = lax.dot_general(picked_ref[b], grid, contract, preferred_element_type=F32)
        reply_ref[b] = jnp.concatenate([reply[0:16, 0:LANES], reply[16:32, LANES:]], axis=0)

    def spread(b):
        tiles = incoming_ref[b].astype(F32)
        lefts = []
        rights = []
        for k, row in enumerate(slot_rows):
            cell = tiles[row : row + 1].astype(jnp.int32)
            section = jnp.broadcast_to(cell >> SECTION_BITS, (8, LANES))
            reply = reply_ref[b, 8 * k : 8 * k + 8, :]
            parts = [jnp.where(section == column * SECTIONS + m, reply, 0.0) for m in range(SECTIONS)]
            highs = [part.astype(BF16).astype(F32) for part in parts]
            lows = [part - high for part, high in zip(parts, highs)]
            lefts.append(jnp.concatenate(highs + lows, axis=0).astype(BF16))
            rights.append(jnp.where(cell_rows == (cell & (SECTION - 1)), 1.0, 0.0).astype(BF16))
        both = lax.dot_general(
            jnp.concatenate(lefts, axis=1), jnp.concatenate(rights, axis=1), contract, preferred_element_type=F32
        )
        sums = [
            both[8 * m : 8 * m + 8] + both[8 * (SECTIONS + m) : 8 * (SECTIONS + m) + 8] for m in range(SECTIONS)
        ]
        total = jnp.concatenate(sums, axis=1)
        sums_ref[b] = total
        if not fold:
            high = total.astype(BF16).astype(F32)
            out_ref[b, 0:16, :] = jnp.concatenate([high, total - high], axis=0).astype(BF16)

    stages = (pick, respond, spread)
    groups = count // GROUP
    for turn in range(groups + len(stages) - 1):
        for lag, stage in enumerate(stages):
            if 0 <= turn - lag < groups:
                for b in range((turn - lag) * GROUP, (turn - lag + 1) * GROUP):
                    stage(b)
    if fold:
        rows = rows_of()
        for pair in range(count // 2):
            packed = []
            for b in (2 * pair, 2 * pair + 1):
                total = sums_ref[b]
                high = total.astype(BF16).astype(F32)
                before = sums_ref[b - 1] if b > 0 else zero
                after = sums_ref[b + 1] if b < count - 1 else zero
                for value, third, seventh in ((high, 0, 1), (total - high, 2, 4), (before, 5, 6)):
                    value = jnp.where(rows == 3, after[third : third + 1], value)
                    packed.append(jnp.where(rows == 7, after[seventh : seventh + 1], value))
            out_ref[48 * pair : 48 * pair + 48, :] = jnp.concatenate(packed, axis=0).astype(BF16)


def total_of(returned_ref, rows):
    total = returned_ref[0, 0:rows, :].astype(F32)
    for q in range(1, returned_ref.shape[0]):
        total = total + returned_ref[q, 0:rows, :].astype(F32)
    return total


def gather_kernel(returned_ref, incoming_ref, gain_ref, fixed_ref, parts_ref, near_ref, far_ref):
    first_half = rows_of() < 4
    factor = fixed_ref[1]
    total = returned_ref[0:48, :].astype(F32)
    for pair in range(1, returned_ref.shape[0] // 48):
        total = total + returned_ref[48 * pair : 48 * pair + 48, :].astype(F32)
    total = total[0:24] + total[24:48]
    ends = [total[row : row + 1] for row in (3, 7, 11, 15, 19, 23)]
    after = jnp.concatenate(ends[0:3] + ends[0:1] + ends[3:6] + ends[0:1], axis=0)
    sources = (total[16:24], total[0:8] + total[8:16], after)
    b = lax.axis_index("work")
    last = lax.axis_size("work") - 1
    upper = near_is_upper("space")
    for n, source in enumerate(sources):
        source = factor * source
        if n == 1:
            density = gain_ref[3]
        else:
            tiles = incoming_ref[jnp.clip(b + n - 1, 0, last)].astype(F32)
            density = tiles[0:8] + tiles[8:16]
        equilibrium = gain_ref[n] * density
        parts_ref[n] = equilibrium
        parts_ref[3 + n] = source
        to_lower = jnp.where(first_half, equilibrium, half(source))
        to_upper = jnp.where(first_half, half(equilibrium), source)
        near_ref[n] = jnp.where(upper, to_upper, to_lower)
        far_ref[n] = jnp.where(upper, to_lower, to_upper)


def second_kernel(
    stay_ref, sides_ref, parts_ref, first_ref, second_ref, fixed_ref,
    pulled_ref, density_ref, payload_ref,
):
    has_right, has_left, _, _ = edges()
    upper = near_is_upper("space")
    first_half = rows_of() < 4
    above = [sides_ref[n] for n in range(5)]
    below = [sides_ref[5 + n] for n in range(5)]
    pulled = {}
    for n, cy in enumerate((-1, 0, 1)):
        equilibrium, source = (parts_ref[n], parts_ref[3 + n])
        right = jnp.where(has_right, jnp.where(upper, first_ref[n], second_ref[n]), 0.0)
        left = jnp.where(has_left, jnp.where(upper, second_ref[n], first_ref[n]), 0.0)
        moved = {
            0: (equilibrium, source),
            1: (jnp.where(first_half, half(equilibrium), half(right)), jnp.where(first_half, half(source), right)),
            -1: (jnp.where(first_half, left, half(equilibrium)), jnp.where(first_half, half(left), half(source))),
        }
        for c in DIRECTIONS:
            if c[1] != cy:
                continue
            shifted, added = moved[c[0]]
            if cy == 0:
                base = stay_ref[{0: 0, 1: 3, -1: 6}[c[0]] + {0: 0, 1: 1, -1: 2}[c[2]]]
            else:
                side = above if cy > 0 else below
                base = side[{0: {0: 0, 1: 1, -1: 2}[c[2]], 1: 3, -1: 4}[c[0]]]
            pulled[c] = along(base + shifted + WEIGHTS[INDEX[c]] * added, c[2])
    pulled = {c: pulled[c] for c in DIRECTIONS}
    density = moment(pulled, [fixed_ref[3 + c] for c in range(3)])
    twice = jnp.concatenate([density, density], axis=0).astype(BF16)
    for pair in range(payload_ref.shape[0] // 16):
        payload_ref[16 * pair : 16 * pair + 16, :] = twice
    for i, c in enumerate(DIRECTIONS):
        pulled_ref[i] = pulled[c]
    density_ref[0] = density


def last_kernel(returned_ref, pulled_ref, density_ref, fixed_ref, out_ref):
    total = total_of(returned_ref, 16)
    rate = fixed_ref[0]
    keep = fixed_ref[2]
    source = fixed_ref[1] * (total[0:8] + total[8:16])
    shared = keep * rate * density_ref[0]
    here = keep * (1.0 - rate)
    for i in range(len(DIRECTIONS)):
        value = here * pulled_ref[i] + shared + WEIGHTS[i] * source
        for x in range(2):
            for s in range(SPECIES):
                row = 4 * x + s
                out_ref[s, i, x] = value[row : row + 1]


def call(kernel, out_shape, in_specs, name, **rest):
    single = not isinstance(out_shape, (tuple, list))
    return pl.pallas_call(
        kernel,
        out_shape=out_shape,
        in_specs=in_specs,
        out_specs=VM if single else tuple(VM for _ in out_shape),
        name=name,
        compiler_params=pltpu.CompilerParams(vmem_limit_bytes=32 * 1024 * 1024),
        **rest,
    )


def swapped(value, axis, odd):
    columns, owners = (lax.axis_size("space"), lax.axis_size("work"))
    pairs = []
    for a in range(columns):
        for b in range(owners):
            at, count = (b, owners) if axis == "work" else (a, columns)
            to = at + (1 if (at % 2 == 0) != odd else -1)
            if 0 <= to < count:
                other = to * owners + b if axis == "space" else a * owners + to
            else:
                other = a * owners + (b ^ 1) if axis == "space" else (a ^ 1) * owners + b
            pairs.append((a * owners + b, other))
    return lax.ppermute(value, ("space", "work"), pairs)


def body(adjoint, velocity, relaxation, uptake, fluid_mask, block_cells, owner_load, response):
    owners = lax.axis_size("work")
    matrices = response.reshape(response.shape[2:])
    speeds = velocity.transpose(0, 2, 1, 3)

    def outside(value):
        return pltpu.with_memory_space_constraint(value, pltpu.HBM)

    def both_ways(near, far, axis):
        return swapped(near, axis, axis == "work"), swapped(far, axis, axis != "work")

    def owner(incoming, densities, fetched, fold):
        return call(
            lambda *refs: owner_kernel(*refs, fold=fold),
            jax.ShapeDtypeStruct((owners * 24, LANES) if fold else (owners, 16, LANES), BF16),
            [VM, VM, VM],
            "owner_fold" if fold else "owner",
            scratch_shapes=[
                pltpu.VMEM((owners, 32, 2 * LANES), BF16),
                pltpu.VMEM((owners, 32, LANES), F32),
                pltpu.VMEM((owners, 8, LANES), F32),
            ],
        )(incoming, densities, fetched)

    def exchange(value):
        return lax.all_to_all(value, "work", split_axis=0, concat_axis=0, tiled=True)

    payload_shape = jax.ShapeDtypeStruct((owners, 16, LANES), BF16)
    middle, near, far, fixed = call(
        arrange_kernel,
        (tile(9), tile(5), tile(5), tile(6)),
        [HBM] * 5,
        "arrange",
        scratch_shapes=[
            pltpu.VMEM(adjoint.shape, F32),
            pltpu.VMEM(speeds.shape, BF16),
            pltpu.VMEM(fluid_mask.shape, jnp.int32),
            pltpu.SMEM(relaxation.shape, F32),
            pltpu.SMEM(uptake.shape, F32),
            pltpu.VMEM((5, 8, LANES), F32),
            pltpu.VMEM((5, 8, LANES), F32),
            pltpu.SemaphoreType.DMA((5,)),
        ],
    )(*map(outside, (adjoint, speeds, fluid_mask, relaxation, uptake)))
    first, second = both_ways(near, far, "space")
    slots, sides = call(
        slots_kernel,
        (tile(owners, rows=16), tile(6)),
        [HBM, HBM, VM],
        "slots",
        scratch_shapes=[
            pltpu.VMEM(block_cells.shape, jnp.int32),
            pltpu.SMEM(owner_load.shape, jnp.int32),
            pltpu.SemaphoreType.DMA((2,)),
        ],
    )(outside(block_cells), outside(owner_load), middle)
    fetched, own = call(
        fetch_kernel,
        (pltpu.VMEM(matrices.shape, BF16), tile(3)),
        [HBM, VM],
        "fetch",
        scratch_shapes=[pltpu.SemaphoreType.DMA((CHUNKS,))],
    )(outside(matrices), middle)
    one, two = call(across_kernel, (tile(7), tile(7)), [VM] * 5, "across")(sides, near, far, first, second)
    one, two = both_ways(one, two, "work")
    stay, third, fourth, gain, payload = call(
        first_kernel, (tile(9), tile(5), tile(5), tile(4), payload_shape), [VM] * 9, "first"
    )(own, near, far, first, second, one, two, fixed, slots)
    incoming = exchange(payload)
    third, fourth = both_ways(third, fourth, "work")
    returned = owner(incoming, payload, fetched, True).reshape(owners, 24, LANES)
    returned = exchange(returned).reshape(-1, LANES)
    parts, near, far = call(gather_kernel, (tile(6), tile(3), tile(3)), [VM] * 4, "gather")(
        returned, incoming, gain, fixed
    )
    first, second = both_ways(near, far, "space")
    fetched, sides = call(
        fetch_again_kernel,
        (pltpu.VMEM(matrices.shape, BF16), tile(10)),
        [HBM, VM, VM],
        "fetch_again",
        scratch_shapes=[pltpu.SemaphoreType.DMA((CHUNKS,))],
    )(outside(matrices), third, fourth)
    pulled, density, payload = call(
        second_kernel, (tile(19), tile(1), jax.ShapeDtypeStruct((owners * 8, LANES), BF16)), [VM] * 6, "second"
    )(stay, sides, parts, first, second, fixed)
    densities = exchange(payload.reshape(owners, 8, LANES)).reshape(-1, LANES)
    returned = exchange(owner(incoming, densities, fetched, False))
    return call(last_kernel, jax.ShapeDtypeStruct(adjoint.shape, F32), [VM] * 4, "last")(
        returned, pulled, density, fixed
    )


def solution(mesh):
    placed = (
        P(None, None, "space", "work", None),
        P(None, "space", "work", None),
        P(),
        P(),
        P("space", "work", None),
        P("space", "work", None, None, None),
        P("space", "work", None),
        P("space", "work", None, None, None, None),
    )
    return jax.shard_map(
        body,
        mesh=mesh,
        in_specs=placed,
        out_specs=P(None, None, "space", "work", None),
        check_vma=False,
    )
```

```python
import jax
import jax.numpy as jnp
from jax import lax
from jax.experimental import pallas as pl
from jax.experimental.pallas import tpu as pltpu
from jax.sharding import PartitionSpec as P

DIRECTIONS = (
    (0, 0, 0),
    (1, 0, 0),
    (-1, 0, 0),
    (0, 1, 0),
    (0, -1, 0),
    (0, 0, 1),
    (0, 0, -1),
    (1, 1, 0),
    (-1, -1, 0),
    (1, -1, 0),
    (-1, 1, 0),
    (1, 0, 1),
    (-1, 0, -1),
    (1, 0, -1),
    (-1, 0, 1),
    (0, 1, 1),
    (0, -1, -1),
    (0, 1, -1),
    (0, -1, 1),
)
WEIGHTS = (1.0 / 3.0,) + (1.0 / 18.0,) * 6 + (1.0 / 36.0,) * 12
INDEX = {c: i for i, c in enumerate(DIRECTIONS)}

MIDDLE = ((0, 0, 0), (0, 0, 1), (0, 0, -1), (0, 1, 0), (0, 1, 1), (0, 1, -1), (0, -1, 0), (0, -1, 1), (0, -1, -1))
PLUS = ((1, 0, 0), (1, 0, 1), (1, 0, -1), (1, 1, 0), (1, -1, 0))
MINUS = ((-1, 0, 0), (-1, 0, 1), (-1, 0, -1), (-1, 1, 0), (-1, -1, 0))
PLACE = {c: n for n, c in enumerate(MIDDLE)}
PLACE.update({c: n for n, c in enumerate(PLUS)})
PLACE.update({c: n for n, c in enumerate(MINUS)})
SPECIES = 3
LANES = 128
F32 = jnp.float32
BF16 = jnp.bfloat16
CHUNKS = 4
GROUP = 4
SECTION_BITS = 6
SECTION = 1 << SECTION_BITS
SECTIONS = LANES // SECTION

VM = pl.BlockSpec(memory_space=pltpu.VMEM)
SM = pl.BlockSpec(memory_space=pltpu.SMEM)
HBM = pl.BlockSpec(memory_space=pltpu.HBM)


def tile(count, dtype=F32, rows=8):
    return jax.ShapeDtypeStruct((count, rows, LANES), dtype)


def rows_of(shape=(8, LANES)):
    return lax.broadcasted_iota(jnp.int32, shape, 0)


def half(value):
    return pltpu.roll(value, 4, 0)


def along(value, step):
    return pltpu.roll(value, (-step) % LANES, 1) if step else value


def per_species(ref):
    species = rows_of() % 4
    out = jnp.zeros((8, LANES), F32)
    for s in range(SPECIES):
        out = jnp.where(species == s, ref[s], out)
    return out


def moment(pulled, speeds):
    density = None
    for c, value in pulled.items():
        factor = 1.0
        drift = None
        for axis in range(3):
            if c[axis]:
                part = speeds[axis] if c[axis] > 0 else -speeds[axis]
                drift = part if drift is None else drift + part
        weight = WEIGHTS[INDEX[c]]
        term = value * weight if drift is None else value * (weight + (3.0 * weight) * drift)
        density = term if density is None else density + term
    return density


def edges():
    a = lax.axis_index("space")
    b = lax.axis_index("work")
    return (a < lax.axis_size("space") - 1, a > 0, b < lax.axis_size("work") - 1, b > 0)


def near_is_upper(axis):
    return lax.axis_index(axis) % 2 == (1 if axis == "work" else 0)


def arrange_kernel(
    field_hbm, velocity_hbm, mask_hbm, relaxation_hbm, uptake_hbm,
    middle_ref, near_ref, far_ref, fixed_ref,
    field_ref, velocity_ref, mask_ref, relaxation_ref, uptake_ref, plus_ref, minus_ref, done,
):
    pairs = (
        (field_hbm, field_ref),
        (velocity_hbm, velocity_ref),
        (mask_hbm, mask_ref),
        (relaxation_hbm, relaxation_ref),
        (uptake_hbm, uptake_ref),
    )
    copies = [pltpu.make_async_copy(source, target, done.at[n]) for n, (source, target) in enumerate(pairs)]
    for copy in copies:
        copy.start()
    for copy in copies:
        copy.wait()
    first_half = rows_of() < 4
    keep = [mask_ref[x].astype(F32) for x in range(2)]
    for group, ref in ((MIDDLE, middle_ref), (PLUS, plus_ref), (MINUS, minus_ref)):
        for n, c in enumerate(group):
            for x in range(2):
                for s in range(SPECIES):
                    row = 4 * x + s
                    ref[n, row : row + 1, :] = field_ref[s, INDEX[c], x]
                ref[n, 4 * x + 3 : 4 * x + 4, :] = keep[x]
    upper = near_is_upper("space")
    for n in range(5):
        plus, minus = (plus_ref[n], minus_ref[n])
        near_ref[n] = jnp.where(upper, minus, plus)
        far_ref[n] = jnp.where(upper, plus, minus)
    fixed_ref[0] = per_species(relaxation_ref)
    fixed_ref[1] = per_species(uptake_ref)
    fixed_ref[2] = jnp.where(first_half, keep[0], keep[1])
    for c in range(3):
        speeds = velocity_ref[c, 0].astype(F32)
        fixed_ref[3 + c] = jnp.where(first_half, speeds[0:1], speeds[1:2])


def start_fetch(response_hbm, response_ref, done):
    parts = done.shape[0]
    each = response_hbm.shape[0] // parts
    copies = [
        pltpu.make_async_copy(
            response_hbm.at[pl.ds(n * each, each)], response_ref.at[pl.ds(n * each, each)], done.at[n]
        )
        for n in range(parts)
    ]
    for copy in copies:
        copy.start()
    return copies


def fetch_kernel(response_hbm, middle_ref, response_ref, own_ref, done):
    copies = start_fetch(response_hbm, response_ref, done)
    own_ref[...] = middle_ref[0:3]
    for copy in copies:
        copy.wait()


def fetch_again_kernel(response_hbm, third_ref, fourth_ref, response_ref, sides_ref, done):
    copies = start_fetch(response_hbm, response_ref, done)
    _, _, has_above, has_below = edges()
    upper_row = near_is_upper("work")
    for n in range(5):
        third, fourth = (third_ref[n], fourth_ref[n])
        sides_ref[n] = jnp.where(has_above, jnp.where(upper_row, third, fourth), 0.0)
        sides_ref[5 + n] = jnp.where(has_below, jnp.where(upper_row, fourth, third), 0.0)
    for copy in copies:
        copy.wait()


def slots_kernel(cells_hbm, load_hbm, middle_ref, slots_ref, sides_ref, cells_ref, load_ref, done):
    pairs = ((cells_hbm, cells_ref), (load_hbm, load_ref))
    copies = [pltpu.make_async_copy(source, target, done.at[n]) for n, (source, target) in enumerate(pairs)]
    for copy in copies:
        copy.start()
    sides_ref[...] = middle_ref[3:9]
    for copy in copies:
        copy.wait()
    rows = rows_of()
    for q in range(slots_ref.shape[0]):
        load = load_ref[0, 0, q]
        cells = cells_ref[0, 0, q].astype(F32)
        live = [jnp.where(k < load, cells[k : k + 1], -1.0) for k in range(4)]
        for n in range(2):
            slots_ref[q, 8 * n : 8 * n + 8, :] = jnp.where(
                rows == 3, live[2 * n], jnp.where(rows == 7, live[2 * n + 1], 0.0)
            )


def across_kernel(sides_ref, near_ref, far_ref, first_ref, second_ref, one_ref, two_ref):
    has_right, has_left, _, _ = edges()
    upper = near_is_upper("space")
    upper_row = near_is_upper("work")
    first_half = rows_of() < 4
    pieces = {}
    for sign in (1, -1):
        p, m = (PLACE[(1, sign, 0)], PLACE[(-1, sign, 0)])
        pieces[sign] = [sides_ref[PLACE[(0, sign, cz)] - 3] for cz in (0, 1, -1)] + [
            jnp.where(
                first_half, jnp.where(upper, near_ref[m], far_ref[m]), jnp.where(upper, far_ref[p], near_ref[p])
            ),
            jnp.where(has_right, jnp.where(upper, first_ref[p], second_ref[p]), 0.0),
            jnp.where(has_left, jnp.where(upper, second_ref[m], first_ref[m]), 0.0),
        ]
    for n in range(6):
        one_ref[n] = jnp.where(upper_row, pieces[-1][n], pieces[1][n])
        two_ref[n] = jnp.where(upper_row, pieces[1][n], pieces[-1][n])


def write_payload(payload_ref, density, slots_ref):
    live = rows_of() % 4 < SPECIES
    high = density.astype(BF16).astype(F32)
    both = jnp.concatenate([jnp.where(live, high, 0.0), jnp.where(live, density - high, 0.0)], axis=0)
    for q in range(payload_ref.shape[0]):
        payload_ref[q] = (both + slots_ref[q]).astype(BF16)


def first_kernel(
    middle_ref, near_ref, far_ref, first_ref, second_ref, one_ref, two_ref, fixed_ref, slots_ref,
    stay_ref, third_ref, fourth_ref, gain_ref, payload_ref,
):
    has_right, has_left, has_above, has_below = edges()
    upper = near_is_upper("space")
    upper_row = near_is_upper("work")
    first_half = rows_of() < 4
    rate = fixed_ref[0]
    keep = fixed_ref[2]
    plus = [jnp.where(upper, far_ref[n], near_ref[n]) for n in range(3)]
    minus = [jnp.where(upper, near_ref[n], far_ref[n]) for n in range(3)]
    right = [jnp.where(has_right, jnp.where(upper, first_ref[n], second_ref[n]), 0.0) for n in range(3)]
    left = [jnp.where(has_left, jnp.where(upper, second_ref[n], first_ref[n]), 0.0) for n in range(3)]
    above = [jnp.where(has_above, jnp.where(upper_row, one_ref[n], two_ref[n]), 0.0) for n in range(6)]
    below = [jnp.where(has_below, jnp.where(upper_row, two_ref[n], one_ref[n]), 0.0) for n in range(6)]
    pulled = {}
    for n, cz in enumerate((0, 1, -1)):
        pulled[(0, 0, cz)] = along(middle_ref[PLACE[(0, 0, cz)]], cz)
        pulled[(1, 0, cz)] = along(jnp.where(first_half, half(plus[n]), half(right[n])), cz)
        pulled[(-1, 0, cz)] = along(jnp.where(first_half, half(left[n]), half(minus[n])), cz)
    for sign, side in ((1, above), (-1, below)):
        for n, cz in enumerate((0, 1, -1)):
            pulled[(0, sign, cz)] = along(side[n], cz)
        pulled[(1, sign, 0)] = jnp.where(first_half, half(side[3]), half(side[4]))
        pulled[(-1, sign, 0)] = jnp.where(first_half, half(side[5]), half(side[3]))
    pulled = {c: pulled[c] for c in DIRECTIONS}
    density = moment(pulled, [fixed_ref[3 + c] for c in range(3)])
    write_payload(payload_ref, density, slots_ref)

    kept = 1.0 - rate
    right_mask = jnp.where(first_half, keep[4:5], right[0][3:4])
    left_mask = jnp.where(first_half, left[0][7:8], keep[0:1])
    here, to_right, to_left = (keep * kept, right_mask * kept, left_mask * kept)
    for n, cz in enumerate((0, 1, -1)):
        stay_ref[n] = here * pulled[(0, 0, cz)]
        stay_ref[3 + n] = to_right * along(right[n], cz)
        stay_ref[6 + n] = to_left * along(left[n], cz)
    sends = {}
    for sign, side in ((1, above), (-1, below)):
        sends[sign] = [here * pulled[(0, sign, cz)] for cz in (0, 1, -1)] + [to_right * side[4], to_left * side[5]]
    for n in range(5):
        third_ref[n] = jnp.where(upper_row, sends[-1][n], sends[1][n])
        fourth_ref[n] = jnp.where(upper_row, sends[1][n], sends[-1][n])
    gain_ref[0] = jnp.where(first_half, below[0][3:4], below[0][7:8]) * rate
    gain_ref[1] = keep * rate
    gain_ref[2] = jnp.where(first_half, above[0][3:4], above[0][7:8]) * rate
    gain_ref[3] = density


def owner_kernel(incoming_ref, density_ref, matrices_ref, out_ref, picked_ref, reply_ref, sums_ref, *, fold):
    count = incoming_ref.shape[0]
    column = jnp.where(rows_of() < 4, 0, 1)
    cell_rows = lax.broadcasted_iota(jnp.int32, (SECTION, LANES), 0)
    contract = (((1,), (1,)), ((), ()))
    zero = jnp.zeros((8, LANES), F32)
    slot_rows = (3, 7, 11, 15)
    def pick(b):
        tiles = incoming_ref[b].astype(F32)
        if fold:
            top = tiles[0:8]
        else:
            pair = density_ref[16 * (b // 2) : 16 * (b // 2) + 16, :].astype(F32)
            top = pair[0:8] if b % 2 == 0 else pair[8:16]
        picked = []
        for row in slot_rows:
            cell = jnp.broadcast_to(tiles[row : row + 1].astype(jnp.int32), (8, LANES))
            found = jnp.take_along_axis(top, cell & (LANES - 1), axis=1, mode="promise_in_bounds")
            picked.append(jnp.where((cell >> 7) == column, found, half(found)))
        upper = jnp.concatenate([picked[0], zero, picked[2], zero], axis=0)
        lower = jnp.concatenate([zero, picked[1], zero, picked[3]], axis=0)
        picked_ref[b] = jnp.concatenate([upper, lower], axis=1).astype(BF16)

    def respond(b):
        top = jnp.concatenate([matrices_ref[b, 0], matrices_ref[b, 1]], axis=1)
        bottom = jnp.concatenate([matrices_ref[b, 2], matrices_ref[b, 3]], axis=1)
        grid = jnp.concatenate([top, bottom], axis=0)
        reply = lax.dot_general(picked_ref[b], grid, contract, preferred_element_type=F32)
        reply_ref[b] = jnp.concatenate([reply[0:16, 0:LANES], reply[16:32, LANES:]], axis=0)

    def spread(b):
        tiles = incoming_ref[b].astype(F32)
        lefts = []
        rights = []
        for k, row in enumerate(slot_rows):
            cell = tiles[row : row + 1].astype(jnp.int32)
            section = jnp.broadcast_to(cell >> SECTION_BITS, (8, LANES))
            reply = reply_ref[b, 8 * k : 8 * k + 8, :]
            parts = [jnp.where(section == column * SECTIONS + m, reply, 0.0) for m in range(SECTIONS)]
            highs = [part.astype(BF16).astype(F32) for part in parts]
            lows = [part - high for part, high in zip(parts, highs)]
            lefts.append(jnp.concatenate(highs + lows, axis=0).astype(BF16))
            rights.append(jnp.where(cell_rows == (cell & (SECTION - 1)), 1.0, 0.0).astype(BF16))
        both = lax.dot_general(
            jnp.concatenate(lefts, axis=1), jnp.concatenate(rights, axis=1), contract, preferred_element_type=F32
        )
        sums = [
            both[8 * m : 8 * m + 8] + both[8 * (SECTIONS + m) : 8 * (SECTIONS + m) + 8] for m in range(SECTIONS)
        ]
        total = jnp.concatenate(sums, axis=1)
        sums_ref[b] = total
        if not fold:
            high = total.astype(BF16).astype(F32)
            out_ref[b, 0:16, :] = jnp.concatenate([high, total - high], axis=0).astype(BF16)

    stages = (pick, respond, spread)
    groups = count // GROUP
    for turn in range(groups + len(stages) - 1):
        for lag, stage in enumerate(stages):
            if 0 <= turn - lag < groups:
                for b in range((turn - lag) * GROUP, (turn - lag + 1) * GROUP):
                    stage(b)
    if fold:
        rows = rows_of()
        for pair in range(count // 2):
            packed = []
            for b in (2 * pair, 2 * pair + 1):
                total = sums_ref[b]
                high = total.astype(BF16).astype(F32)
                before = sums_ref[b - 1] if b > 0 else zero
                after = sums_ref[b + 1] if b < count - 1 else zero
                for value, third, seventh in ((high, 0, 1), (total - high, 2, 4), (before, 5, 6)):
                    value = jnp.where(rows == 3, after[third : third + 1], value)
                    packed.append(jnp.where(rows == 7, after[seventh : seventh + 1], value))
            out_ref[48 * pair : 48 * pair + 48, :] = jnp.concatenate(packed, axis=0).astype(BF16)


def total_of(returned_ref, rows):
    total = returned_ref[0, 0:rows, :].astype(F32)
    for q in range(1, returned_ref.shape[0]):
        total = total + returned_ref[q, 0:rows, :].astype(F32)
    return total


def gather_kernel(returned_ref, incoming_ref, gain_ref, fixed_ref, parts_ref, near_ref, far_ref):
    first_half = rows_of() < 4
    factor = fixed_ref[1]
    total = returned_ref[0:48, :].astype(F32)
    for pair in range(1, returned_ref.shape[0] // 48):
        total = total + returned_ref[48 * pair : 48 * pair + 48, :].astype(F32)
    total = total[0:24] + total[24:48]
    ends = [total[row : row + 1] for row in (3, 7, 11, 15, 19, 23)]
    after = jnp.concatenate(ends[0:3] + ends[0:1] + ends[3:6] + ends[0:1], axis=0)
    sources = (total[16:24], total[0:8] + total[8:16], after)
    b = lax.axis_index("work")
    last = lax.axis_size("work") - 1
    upper = near_is_upper("space")
    for n, source in enumerate(sources):
        source = factor * source
        if n == 1:
            density = gain_ref[3]
        else:
            tiles = incoming_ref[jnp.clip(b + n - 1, 0, last)].astype(F32)
            density = tiles[0:8] + tiles[8:16]
        equilibrium = gain_ref[n] * density
        parts_ref[n] = equilibrium
        parts_ref[3 + n] = source
        to_lower = jnp.where(first_half, equilibrium, half(source))
        to_upper = jnp.where(first_half, half(equilibrium), source)
        near_ref[n] = jnp.where(upper, to_upper, to_lower)
        far_ref[n] = jnp.where(upper, to_lower, to_upper)


def second_kernel(
    stay_ref, sides_ref, parts_ref, first_ref, second_ref, fixed_ref,
    pulled_ref, density_ref, payload_ref,
):
    has_right, has_left, _, _ = edges()
    upper = near_is_upper("space")
    first_half = rows_of() < 4
    above = [sides_ref[n] for n in range(5)]
    below = [sides_ref[5 + n] for n in range(5)]
    pulled = {}
    for n, cy in enumerate((-1, 0, 1)):
        equilibrium, source = (parts_ref[n], parts_ref[3 + n])
        right = jnp.where(has_right, jnp.where(upper, first_ref[n], second_ref[n]), 0.0)
        left = jnp.where(has_left, jnp.where(upper, second_ref[n], first_ref[n]), 0.0)
        moved = {
            0: (equilibrium, source),
            1: (jnp.where(first_half, half(equilibrium), half(right)), jnp.where(first_half, half(source), right)),
            -1: (jnp.where(first_half, left, half(equilibrium)), jnp.where(first_half, half(left), half(source))),
        }
        for c in DIRECTIONS:
            if c[1] != cy:
                continue
            shifted, added = moved[c[0]]
            if cy == 0:
                base = stay_ref[{0: 0, 1: 3, -1: 6}[c[0]] + {0: 0, 1: 1, -1: 2}[c[2]]]
            else:
                side = above if cy > 0 else below
                base = side[{0: {0: 0, 1: 1, -1: 2}[c[2]], 1: 3, -1: 4}[c[0]]]
            pulled[c] = along(base + shifted + WEIGHTS[INDEX[c]] * added, c[2])
    pulled = {c: pulled[c] for c in DIRECTIONS}
    density = moment(pulled, [fixed_ref[3 + c] for c in range(3)])
    twice = jnp.concatenate([density, density], axis=0).astype(BF16)
    for pair in range(payload_ref.shape[0] // 16):
        payload_ref[16 * pair : 16 * pair + 16, :] = twice
    for i, c in enumerate(DIRECTIONS):
        pulled_ref[i] = pulled[c]
    density_ref[0] = density


def last_kernel(returned_ref, pulled_ref, density_ref, fixed_ref, out_ref):
    total = total_of(returned_ref, 16)
    rate = fixed_ref[0]
    keep = fixed_ref[2]
    source = fixed_ref[1] * (total[0:8] + total[8:16])
    shared = keep * rate * density_ref[0]
    here = keep * (1.0 - rate)
    for i in range(len(DIRECTIONS)):
        value = here * pulled_ref[i] + shared + WEIGHTS[i] * source
        for x in range(2):
            for s in range(SPECIES):
                row = 4 * x + s
                out_ref[s, i, x] = value[row : row + 1]


def call(kernel, out_shape, in_specs, name, **rest):
    single = not isinstance(out_shape, (tuple, list))
    return pl.pallas_call(
        kernel,
        out_shape=out_shape,
        in_specs=in_specs,
        out_specs=VM if single else tuple(VM for _ in out_shape),
        name=name,
        compiler_params=pltpu.CompilerParams(vmem_limit_bytes=32 * 1024 * 1024),
        **rest,
    )


def swapped(value, axis, odd):
    columns, owners = (lax.axis_size("space"), lax.axis_size("work"))
    pairs = []
    for a in range(columns):
        for b in range(owners):
            at, count = (b, owners) if axis == "work" else (a, columns)
            to = at + (1 if (at % 2 == 0) != odd else -1)
            if 0 <= to < count:
                other = to * owners + b if axis == "space" else a * owners + to
            else:
                other = a * owners + (b ^ 1) if axis == "space" else (a ^ 1) * owners + b
            pairs.append((a * owners + b, other))
    return lax.ppermute(value, ("space", "work"), pairs)


def body(adjoint, velocity, relaxation, uptake, fluid_mask, block_cells, owner_load, response):
    owners = lax.axis_size("work")
    matrices = response.reshape(response.shape[2:])
    speeds = velocity.transpose(0, 2, 1, 3)

    def outside(value):
        return pltpu.with_memory_space_constraint(value, pltpu.HBM)

    def both_ways(near, far, axis):
        return swapped(near, axis, axis == "work"), swapped(far, axis, axis != "work")

    def owner(incoming, densities, fetched, fold):
        return call(
            lambda *refs: owner_kernel(*refs, fold=fold),
            jax.ShapeDtypeStruct((owners * 24, LANES) if fold else (owners, 16, LANES), BF16),
            [VM, VM, VM],
            "owner_fold" if fold else "owner",
            scratch_shapes=[
                pltpu.VMEM((owners, 32, 2 * LANES), BF16),
                pltpu.VMEM((owners, 32, LANES), F32),
                pltpu.VMEM((owners, 8, LANES), F32),
            ],
        )(incoming, densities, fetched)

    def exchange(value):
        return lax.all_to_all(value, "work", split_axis=0, concat_axis=0, tiled=True)

    payload_shape = jax.ShapeDtypeStruct((owners, 16, LANES), BF16)
    middle, near, far, fixed = call(
        arrange_kernel,
        (tile(9), tile(5), tile(5), tile(6)),
        [HBM] * 5,
        "arrange",
        scratch_shapes=[
            pltpu.VMEM(adjoint.shape, F32),
            pltpu.VMEM(speeds.shape, BF16),
            pltpu.VMEM(fluid_mask.shape, jnp.int32),
            pltpu.SMEM(relaxation.shape, F32),
            pltpu.SMEM(uptake.shape, F32),
            pltpu.VMEM((5, 8, LANES), F32),
            pltpu.VMEM((5, 8, LANES), F32),
            pltpu.SemaphoreType.DMA((5,)),
        ],
    )(*map(outside, (adjoint, speeds, fluid_mask, relaxation, uptake)))
    first, second = both_ways(near, far, "space")
    slots, sides = call(
        slots_kernel,
        (tile(owners, rows=16), tile(6)),
        [HBM, HBM, VM],
        "slots",
        scratch_shapes=[
            pltpu.VMEM(block_cells.shape, jnp.int32),
            pltpu.SMEM(owner_load.shape, jnp.int32),
            pltpu.SemaphoreType.DMA((2,)),
        ],
    )(outside(block_cells), outside(owner_load), middle)
    fetched, own = call(
        fetch_kernel,
        (pltpu.VMEM(matrices.shape, BF16), tile(3)),
        [HBM, VM],
        "fetch",
        scratch_shapes=[pltpu.SemaphoreType.DMA((CHUNKS,))],
    )(outside(matrices), middle)
    one, two = call(across_kernel, (tile(6), tile(6)), [VM] * 5, "across")(sides, near, far, first, second)
    one, two = both_ways(one, two, "work")
    stay, third, fourth, gain, payload = call(
        first_kernel, (tile(9), tile(5), tile(5), tile(4), payload_shape), [VM] * 9, "first"
    )(own, near, far, first, second, one, two, fixed, slots)
    incoming = exchange(payload)
    third, fourth = both_ways(third, fourth, "work")
    returned = owner(incoming, payload, fetched, True).reshape(owners, 24, LANES)
    returned = exchange(returned).reshape(-1, LANES)
    parts, near, far = call(gather_kernel, (tile(6), tile(3), tile(3)), [VM] * 4, "gather")(
        returned, incoming, gain, fixed
    )
    first, second = both_ways(near, far, "space")
    fetched, sides = call(
        fetch_again_kernel,
        (pltpu.VMEM(matrices.shape, BF16), tile(10)),
        [HBM, VM, VM],
        "fetch_again",
        scratch_shapes=[pltpu.SemaphoreType.DMA((CHUNKS,))],
    )(outside(matrices), third, fourth)
    pulled, density, payload = call(
        second_kernel, (tile(19), tile(1), jax.ShapeDtypeStruct((owners * 8, LANES), BF16)), [VM] * 6, "second"
    )(stay, sides, parts, first, second, fixed)
    densities = exchange(payload.reshape(owners, 8, LANES)).reshape(-1, LANES)
    returned = exchange(owner(incoming, densities, fetched, False))
    return call(last_kernel, jax.ShapeDtypeStruct(adjoint.shape, F32), [VM] * 4, "last")(
        returned, pulled, density, fixed
    )


def solution(mesh):
    placed = (
        P(None, None, "space", "work", None),
        P(None, "space", "work", None),
        P(),
        P(),
        P("space", "work", None),
        P("space", "work", None, None, None),
        P("space", "work", None),
        P("space", "work", None, None, None, None),
    )
    return jax.shard_map(
        body,
        mesh=mesh,
        in_specs=placed,
        out_specs=P(None, None, "space", "work", None),
        check_vma=False,
    )
```
